32 devices in a mesh: groups: 2 (over x), row: 8 (over z, y), col: 2 (over core).
Axes of the slice: x: 2, y: 2, z: 4, core: 2. Of those that a mesh axis runs over, the one named last changes fastest.
Arguments:
- hamiltonian: float32 [192, 7, 128, 128], P(('groups', 'row'), None, 'col'), parts along dimension 0, may hold values from -2.5 to 2.5, as said below
- bounds: float32 [4], P('groups'), parts along dimension 0, may hold values from 5 to 6
- block_reach: int32 [192], P(('groups', 'row')), parts along dimension 0, may hold values from 2 to 6, as said below
- branch_flags: int32 [2], P('groups'), parts along dimension 0, may hold values from 0 to 1
Outputs:
- density: float32 [192, 7, 128, 128], P(('groups', 'row'), None, 'col'), parts along dimension 0
- occupancy: float32 [2], P('groups'), parts along dimension 0
The draws below stay inside these ranges and needn't reach their ends.
There are 2 independent parts, one for each index of `groups`. The reference program is written for one: setup_inputs(seed, part) draws one part's arguments, and reference() takes and returns one part's arrays. A program takes and returns all parts, laid end to end along the dimension named above; each array names one. Nothing has to cross between parts.
Inputs may be any that keep to these rules, and one draw needn't show every extreme that they name: The diagonal blocks hamiltonian[i, 0] are symmetric; the spectrum of the full symmetric matrix lies between -bounds[0] and bounds[1]. `block_reach`: in every draw some block rows reach 6.
All inputs are finite; a program needn't handle non-finite values.
Results may differ from the reference program's by a relative error of at most 0.005.
Values may be sent and summed in bfloat16 or wider, within the bound.
No kernel may reach another device: no remote copies, remote signals or barrier semaphores. Data moves between devices by JAX's collectives and lax.ppermute only.
A program may use at most 64 MiB of HBM per device.

```python
import math
import jax
import jax.numpy as jnp
from jax import lax

B = 128
W = 6
ITERS = 1
NB = 96


def draw_hamiltonian(key, part):
    key = jax.random.fold_in(key, 11)
    key_coupling, key_levels, key_scale, key_offset, key_sign, key_freq, key_phase = jax.random.split(key, 7)
    array_shape = (NB, W + 1, B, B)
    spread = 2.0 / math.sqrt((2 * W + 1) * B)
    weight_total = 1 + 2 * sum(((d + 1) ** 2 for d in range(1, W + 1)))
    norm_factor = (2 * W + 1) / weight_total
    offset_scale = jnp.sqrt(norm_factor * (jnp.arange(W + 1, dtype=jnp.float32) + 1.0) ** 2)
    coupling = jax.random.normal(key_coupling, array_shape, jnp.float32)
    coupling = coupling * spread * offset_scale[None, :, None, None]
    diag_block = 0.5 * (coupling[:, 0] + jnp.swapaxes(coupling[:, 0], 1, 2))
    position = (jnp.arange(NB, dtype=jnp.float32)[:, None] * B + jnp.arange(B, dtype=jnp.float32)[None, :]) / (NB * B)
    level_sign = jnp.where(jax.random.uniform(key_sign, (), jnp.float32) < 0.5, -1.0, 1.0)
    level_offset = level_sign * jax.random.uniform(key_offset, (), jnp.float32, 0.35, 0.5)
    frequency = jax.random.uniform(key_freq, (), jnp.float32, 0.7, 1.7)
    phase = jax.random.uniform(key_phase, (), jnp.float32, -math.pi, math.pi)
    smooth = 0.3 * jnp.sin(2.0 * math.pi * frequency * position + phase)
    energies = level_offset + (-0.5 + 1.0 * position) + smooth + jax.random.uniform(key_levels, (NB, B), jnp.float32, -0.2, 0.2)
    identity = jnp.eye(B, dtype=jnp.float32)
    diag_block = diag_block * (1.0 - identity) + energies[:, :, None] * identity
    return coupling.at[:, 0].set(diag_block)


def draw_block_reach(key, part):
    key = jax.random.fold_in(key, 5)
    key_base, key_wide, key_spot = jax.random.split(key, 3)
    base_reach = jax.random.randint(key_base, (NB,), W // 3, W + 1)
    widest = jax.random.randint(key_wide, (NB,), 0, 2) == 0
    chosen = jax.random.randint(key_spot, (), 0, NB)
    row_ids = jnp.arange(NB, dtype=jnp.int32)
    return jnp.where(widest | (row_ids == chosen), W, base_reach).astype(jnp.int32)


def setup_inputs(seed: int = 0, part: int = 0) -> dict:
    arg_keys = jax.random.split(jax.random.key(seed), 5)
    own_keys = jax.random.split(jax.random.fold_in(arg_keys[4], part), 5)
    return {
        "hamiltonian": draw_hamiltonian(jax.random.fold_in(jax.random.fold_in(arg_keys[4], part), 71), part),
        "bounds": jnp.clip(jax.random.uniform(own_keys[1], (2,), jnp.float32, 5.0, 6.0), 5.0, 6.0),
        "block_reach": draw_block_reach(jax.random.fold_in(jax.random.fold_in(arg_keys[4], part), 71), part),
        "branch_flags": jax.random.randint(own_keys[3], (ITERS,), 0, 2).astype(jnp.int32),
    }


def band_square(band):
    row_count = band.shape[0]
    extended = jnp.pad(band, ((W, W), (0, 0), (0, 0), (0, 0)))
    skewed = jnp.stack([extended[W - m: W - m + row_count + W, m] for m in range(W + 1)], axis=1)
    lower_part = jnp.stack([jnp.swapaxes(extended[W - k: W - k + row_count, k], 1, 2) for k in range(1, W + 1)], axis=1)
    left_blocks = jnp.concatenate([band[:, ::-1], lower_part], axis=1)
    products = []
    for d in range(W + 1):
        total = jnp.einsum("rmpq,rmqs->rps", left_blocks[:, W - d: 2 * W - d + 1], skewed[d: d + row_count], precision=lax.Precision.HIGHEST)
        if d < W:
            total = total + jnp.einsum("repq,resq->rps", band[:, d + 1:], extended[W + d: W + d + row_count, 1: W - d + 1], precision=lax.Precision.HIGHEST)
        products.append(total)
    return jnp.stack(products, axis=1)


def reference(hamiltonian, bounds, block_reach, branch_flags):
    offsets = jnp.arange(W + 1, dtype=jnp.int32)
    row_ids = jnp.arange(NB, dtype=jnp.int32)
    kept_mask = (offsets[None, :] <= block_reach[:, None]) & (row_ids[:, None] + offsets[None, :] < NB)
    orbital = jnp.arange(B, dtype=jnp.int32)
    unit_diag = jnp.where((offsets[:, None, None] == 0) & (orbital[None, :, None] == orbital[None, None, :]), 1.0, 0.0).astype(jnp.float32)
    spectrum_low = -bounds[0]
    spectrum_high = bounds[1]
    start_band = (spectrum_high * unit_diag[None] - hamiltonian) / (spectrum_high - spectrum_low)
    current = jnp.where(kept_mask[:, :, None, None], start_band, 0.0).astype(jnp.bfloat16)
    final_band = current.astype(jnp.float32)
    occupied = []
    for n in range(ITERS):
        previous = current.astype(jnp.float32)
        square = jnp.where(kept_mask[:, :, None, None], band_square(previous), 0.0)
        updated = jnp.where(branch_flags[n] == 1, square, 2.0 * previous - square)
        diagonal_sum = jnp.sum(jnp.diagonal(updated[:, 0], axis1=1, axis2=2))
        occupied.append(diagonal_sum / (NB * B))
        final_band = updated
        current = updated.astype(jnp.bfloat16)
    return final_band, jnp.stack(occupied)
```

```python
import functools

import jax
import jax.numpy as jnp
from jax import lax
from jax.experimental import pallas as pl
from jax.experimental.pallas import tpu as pltpu
from jax.sharding import PartitionSpec as P

SMEM = pl.BlockSpec(memory_space=pltpu.SMEM)
VMEM = pl.BlockSpec(memory_space=pltpu.VMEM)
ANY = pl.BlockSpec(memory_space=pl.ANY)
F32 = jnp.float32
BF16 = jnp.bfloat16
MIB = 1 << 20


def tail_blocks(rows, width):
    return [(rows - m, d) for m in range(1, width + 1) for d in range(m, width + 1)]


def head_blocks(width):
    return [(m, d) for m in range(width) for d in range(width - m)]


def runs(blocks):
    out = []
    for place, (row, d) in enumerate(blocks):
        if out and out[-1][0] == row:
            out[-1][2] += 1
        else:
            out.append([row, d, 1, place])
    return out


def is_kept(reach_ref, row, d, first_row, total_rows):
    return (d <= reach_ref[row]) & (first_row + row + d < total_rows)


def start_block(h, d, kept, bounds_ref, on_diag):
    high = bounds_ref[1]
    scale = jnp.where(kept, 1.0, 0.0) / (high + bounds_ref[0])
    if d == 0:
        return ((jnp.where(on_diag, high, 0.0) - h) * scale).astype(BF16)
    return (h * -scale).astype(BF16)


def diag_mask(half, size):
    rows = lax.broadcasted_iota(jnp.int32, (half, size), 0) + lax.axis_index("col") * half
    return lax.broadcasted_iota(jnp.int32, (half, size), 1) == rows


def pack_kernel(dims, reach_ref, bounds_ref, h_ref, tail_ref, head_ref, buf, sems):
    rows, width, half, size = dims
    first_row = lax.axis_index("row") * rows
    total_rows = lax.axis_size("row") * rows
    on_diag = diag_mask(half, size)
    jobs = [(out, run) for out, blocks in ((tail_ref, tail_blocks(rows, width)), (head_ref, head_blocks(width)))
            for run in runs(blocks)]
    copies = []
    at = 0
    for n, (out, (row, d, count, place)) in enumerate(jobs):
        copy = pltpu.make_async_copy(h_ref.at[row, pl.ds(d, count)], buf.at[pl.ds(at, count)], sems.at[n])
        copy.start()
        copies.append((copy, at))
        at += count
    for (out, (row, d, count, place)), (copy, at) in zip(jobs, copies):
        copy.wait()
        for e in range(count):
            kept = is_kept(reach_ref, row, d + e, first_row, total_rows)
            out[place + e] = start_block(buf[at + e], d + e, kept, bounds_ref, on_diag)


def start_kernel(dims, reach_ref, bounds_ref, flag_ref, h_ref, after_ref, x_ref, part_ref):
    rows, width, half, size = dims
    first_row = lax.axis_index("row") * rows
    total_rows = lax.axis_size("row") * rows
    on_diag = diag_mask(half, size)
    count = h_ref.shape[0]
    step = pl.program_id(0)

    def fold(block):
        return jnp.sum(block.reshape(half // 8, 8, size), axis=0)

    diag = jnp.zeros((8, size), F32)
    once = jnp.zeros((8, size), F32)
    twice = jnp.zeros((8, size), F32)
    for e in range(count):
        row = step * count + e
        for d in range(width + 1):
            kept = is_kept(reach_ref, row, d, first_row, total_rows)
            x = start_block(h_ref[e, d], d, kept, bounds_ref, on_diag)
            x_ref[e, d] = x
            wide = x.astype(F32)
            if d == 0:
                diag = diag + fold(jnp.where(on_diag, wide, 0.0))
                once = once + fold(wide * wide)
            else:
                twice = twice + fold(wide * wide)
    norm = once + 2.0 * twice
    part = jnp.where(flag_ref[0] == 1, norm, 2.0 * diag - norm)

    @pl.when(step == 0)
    def _():
        part_ref[...] = part

    @pl.when(step > 0)
    def _():
        part_ref[...] += part


def strips(rows, width):
    out = []
    for j in range(0, rows + width, 2):
        cols = list(range(j, min(j + 2, rows + width)))
        i_lo, i_hi = max(0, j - width), min(rows - 1, cols[-1])
        k_lo = max(0, j - width)
        k_hi = min(rows + width - 1 if j < rows else rows - 1, cols[-1] + width, i_hi + width)
        out.append((cols, i_lo, i_hi, k_lo, k_hi))
    return out


def inner_kernel(dims, reach_ref, flag_ref, mine_ref, other_ref, out_ref, full, left):
    rows, width, half, size = dims
    column = lax.axis_index("col")
    first_row = lax.axis_index("row") * rows
    total_rows = lax.axis_size("row") * rows
    mine = pl.multiple_of(column * half, half)
    other = pl.multiple_of((1 - column) * half, half)
    zero_full = jnp.zeros((size, size), BF16)
    zero_left = jnp.zeros((half, size), BF16)

    def block(n):
        return pl.ds(n * size, size)

    for k in range(rows):
        for d in range(width + 1):
            full[pl.ds(k * size + mine, half), block(k + d)] = mine_ref[k, d]
            full[pl.ds(k * size + other, half), block(k + d)] = other_ref[k, d]
    have_full = {(k, k + d) for k in range(rows) for d in range(width + 1)}
    for j in range(rows):
        for d in range(1, width + 1):
            full[block(j + d), block(j)] = full[block(j), block(j + d)].T
            have_full.add((j + d, j))
    need_full, need_left = set(), set()
    for cols, i_lo, i_hi, k_lo, k_hi in strips(rows, width):
        need_full |= {(k, j) for k in range(k_lo, k_hi + 1) for j in cols}
        need_left |= {(i, k) for i in range(i_lo, i_hi + 1) for k in range(k_lo, k_hi + 1)}
    for k, j in sorted(need_full - have_full):
        full[block(k), block(j)] = zero_full
    for i, k in sorted(need_left):
        if k < i - width or k > i + width:
            piece = zero_left
        elif k >= i:
            piece = mine_ref[i, k - i]
        else:
            piece = full[pl.ds(i * size + mine, half), block(k)]
        left[pl.ds(i * half, half), block(k)] = piece

    sign = jnp.where(flag_ref[0] == 1, 1.0, -1.0)
    twice = jnp.where(flag_ref[0] == 1, 0.0, 2.0)
    for cols, i_lo, i_hi, k_lo, k_hi in strips(rows, width):
        depth = pl.ds(k_lo * size, (k_hi - k_lo + 1) * size)
        square = jnp.dot(
            left[pl.ds(i_lo * half, (i_hi - i_lo + 1) * half), depth],
            full[depth, pl.ds(cols[0] * size, len(cols) * size)],
            preferred_element_type=F32,
        )
        for n, j in enumerate(cols):
            for i in range(max(i_lo, j - width), min(i_hi, j) + 1):
                d = j - i
                kept = is_kept(reach_ref, i, d, first_row, total_rows)
                part = square[(i - i_lo) * half : (i - i_lo + 1) * half, n * size : (n + 1) * size]
                out_ref[i, d] = part * jnp.where(kept, sign, 0.0) + twice * mine_ref[i, d].astype(F32)


def halo_kernel(
    dims, reach_ref, flag_ref, above_mine, above_other, below_mine, below_other, own_tail, base_ref, out_ref,
    above, above_t, above_left, below, tail_left, held, in_sems, out_sems,
):
    rows, width, half, size = dims
    column = lax.axis_index("col")
    first_row = lax.axis_index("row") * rows
    total_rows = lax.axis_size("row") * rows
    mine = pl.multiple_of(column * half, half)
    other = pl.multiple_of((1 - column) * half, half)
    tails, heads = tail_blocks(rows, width), head_blocks(width)

    copies = []
    jobs = [(run, run[3]) for run in runs(heads)] + [(run, len(heads) + run[3]) for run in runs(tails)]
    for n, ((row, d, count, _), at) in enumerate(jobs):
        copy = pltpu.make_async_copy(base_ref.at[row, pl.ds(d, count)], held.at[pl.ds(at, count)], in_sems.at[n])
        copy.start()
        copies.append(copy)

    def block(n):
        return pl.ds(n * size, size)

    zero_full = jnp.zeros((size, size), BF16)
    zero_left = jnp.zeros((half, size), BF16)
    have = set()
    for n, (row, d) in enumerate(tails):
        k, j = row - rows + width, row + d - rows
        above[pl.ds(k * size + mine, half), block(j)] = above_mine[n]
        above[pl.ds(k * size + other, half), block(j)] = above_other[n]
        tail_left[pl.ds(k * half, half), block(j)] = own_tail[n]
        have.add((k, j))
    for k in range(width):
        for j in range(width):
            if (k, j) not in have:
                above[block(k), block(j)] = zero_full
                above_left[pl.ds(j * half, half), block(k)] = zero_left
                tail_left[pl.ds(k * half, half), block(j)] = zero_left
    for k, j in sorted(have):
        above_t[block(j), block(k)] = above[block(k), block(j)].T
        above_left[pl.ds(j * half, half), block(k)] = above_t[pl.ds(j * size + mine, half), block(k)]
    for n, (k, d) in enumerate(heads):
        below[pl.ds(k * size + mine, half), block(k + d)] = below_mine[n]
        below[pl.ds(k * size + other, half), block(k + d)] = below_other[n]
    for k, d in heads:
        if d:
            below[block(k + d), block(k)] = below[block(k), block(k + d)].T
    first = jnp.dot(above_left[...], above[...], preferred_element_type=F32)
    second = jnp.dot(tail_left[...], below[...], preferred_element_type=F32)

    sign = jnp.where(flag_ref[0] == 1, 1.0, -1.0)
    backs = []
    for n, ((row, d, count, _), at) in enumerate(jobs):
        copies[n].wait()
        for e in range(count):
            if n < len(runs(heads)):
                i, j, square = row, row + d + e, first
            else:
                i, j, square = row - rows + width, row + d + e - rows, second
            kept = is_kept(reach_ref, row, d + e, first_row, total_rows)
            part = square[i * half : (i + 1) * half, j * size : (j + 1) * size]
            held[at + e] = held[at + e] + part * jnp.where(kept, sign, 0.0)
        copy = pltpu.make_async_copy(held.at[pl.ds(at, count)], out_ref.at[row, pl.ds(d, count)], out_sems.at[n])
        copy.start()
        backs.append(copy)
    for copy in backs:
        copy.wait()


def per_device(hamiltonian, bounds, block_reach, branch_flags):
    rows, offsets, half, size = hamiltonian.shape
    width = offsets - 1
    dims = (rows, width, half, size)
    halo = len(head_blocks(width))
    count = lax.axis_size("row")
    down = [(i, i + 1) for i in range(count - 1)]
    up = [(i + 1, i) for i in range(count - 1)]
    swap = [(0, 1), (1, 0)]
    packed = jax.ShapeDtypeStruct((halo, half, size), BF16)
    runs_count = 2 * width

    tail, head = pl.pallas_call(
        functools.partial(pack_kernel, dims),
        out_shape=(packed, packed),
        in_specs=[SMEM, SMEM, ANY],
        out_specs=(VMEM, VMEM),
        scratch_shapes=[pltpu.VMEM((2 * halo, half, size), F32), pltpu.SemaphoreType.DMA((runs_count,))],
        compiler_params=pltpu.CompilerParams(vmem_limit_bytes=8 * MIB),
        name="pack",
    )(block_reach, bounds, hamiltonian)
    above_mine = lax.ppermute(tail, "row", down)
    below_mine = lax.ppermute(head, "row", up)

    per_step = 3 if rows % 3 == 0 else 1
    current, part = pl.pallas_call(
        functools.partial(start_kernel, dims),
        grid=(rows // per_step,),
        out_shape=(jax.ShapeDtypeStruct(hamiltonian.shape, BF16), jax.ShapeDtypeStruct((8, size), F32)),
        in_specs=[SMEM, SMEM, SMEM, pl.BlockSpec((per_step, offsets, half, size), lambda s: (s, 0, 0, 0)), ANY],
        out_specs=(
            pl.BlockSpec((per_step, offsets, half, size), lambda s: (s, 0, 0, 0)),
            pl.BlockSpec((8, size), lambda s: (0, 0)),
        ),
        compiler_params=pltpu.CompilerParams(vmem_limit_bytes=16 * MIB),
        cost_estimate=pl.CostEstimate(flops=4 * hamiltonian.size, bytes_accessed=6 * hamiltonian.size, transcendentals=0),
        name="start",
    )(block_reach, bounds, branch_flags, hamiltonian, tail)
    swapped = lax.ppermute(current, "col", swap)
    trace = lax.psum(part, ("row", "col"))

    products = rows * sum(2 * width + 1 - d for d in range(width + 1))
    base = pl.pallas_call(
        functools.partial(inner_kernel, dims),
        out_shape=jax.ShapeDtypeStruct(hamiltonian.shape, F32),
        in_specs=[SMEM, SMEM, VMEM, VMEM],
        out_specs=VMEM,
        scratch_shapes=[
            pltpu.VMEM(((rows + width) * size, (rows + width) * size), BF16),
            pltpu.VMEM((rows * half, (rows + width) * size), BF16),
        ],
        compiler_params=pltpu.CompilerParams(vmem_limit_bytes=40 * MIB),
        cost_estimate=pl.CostEstimate(
            flops=2 * products * half * size * size, bytes_accessed=8 * hamiltonian.size, transcendentals=0
        ),
        name="inner",
    )(block_reach, branch_flags, current, swapped)

    above_other = lax.ppermute(above_mine, "col", swap)
    below_other = lax.ppermute(below_mine, "col", swap)
    density = pl.pallas_call(
        functools.partial(halo_kernel, dims),
        out_shape=jax.ShapeDtypeStruct(hamiltonian.shape, F32),
        in_specs=[SMEM, SMEM, VMEM, VMEM, VMEM, VMEM, VMEM, ANY],
        out_specs=ANY,
        input_output_aliases={7: 0},
        scratch_shapes=[
            pltpu.VMEM((width * size, width * size), BF16),
            pltpu.VMEM((width * size, width * size), BF16),
            pltpu.VMEM((width * half, width * size), BF16),
            pltpu.VMEM((width * size, width * size), BF16),
            pltpu.VMEM((width * half, width * size), BF16),
            pltpu.VMEM((2 * halo, half, size), F32),
            pltpu.SemaphoreType.DMA((runs_count,)),
            pltpu.SemaphoreType.DMA((runs_count,)),
        ],
        compiler_params=pltpu.CompilerParams(vmem_limit_bytes=24 * MIB),
        name="halo",
    )(block_reach, branch_flags, above_mine, above_other, below_mine, below_other, tail, base)
    occupancy = jnp.sum(trace) / (count * rows * size)
    return density, occupancy.reshape(1)


def solution(mesh):
    placed = (
        P(("groups", "row"), None, "col", None),
        P("groups"),
        P(("groups", "row")),
        P("groups"),
    )
    return jax.shard_map(
        per_device,
        mesh=mesh,
        in_specs=placed,
        out_specs=(P(("groups", "row"), None, "col", None), P("groups")),
        check_vma=False,
    )
```

```python
import functools

import jax
import jax.numpy as jnp
from jax import lax
from jax.experimental import pallas as pl
from jax.experimental.pallas import tpu as pltpu
from jax.sharding import PartitionSpec as P

SMEM = pl.BlockSpec(memory_space=pltpu.SMEM)
VMEM = pl.BlockSpec(memory_space=pltpu.VMEM)
ANY = pl.BlockSpec(memory_space=pl.ANY)
HBM = pl.BlockSpec(memory_space=pltpu.HBM)
F32 = jnp.float32
BF16 = jnp.bfloat16
MIB = 1 << 20
SMALL = pl.CostEstimate(flops=1, bytes_accessed=1, transcendentals=0)


def tail_blocks(rows, width):
    return [(rows - m, d) for m in range(1, width + 1) for d in range(m, width + 1)]


def head_blocks(width):
    return [(m, d) for m in range(width) for d in range(width - m)]


def runs(blocks):
    out = []
    for place, (row, d) in enumerate(blocks):
        if out and out[-1][0] == row:
            out[-1][2] += 1
        else:
            out.append([row, d, 1, place])
    return out


def is_kept(reach_ref, row, d, first_row, total_rows):
    return (d <= reach_ref[row]) & (first_row + row + d < total_rows)


def start_block(h, d, kept, bounds_ref, on_diag):
    high = bounds_ref[1]
    scale = jnp.where(kept, 1.0, 0.0) / (high + bounds_ref[0])
    if d == 0:
        return ((jnp.where(on_diag, high, 0.0) - h) * scale).astype(BF16)
    return (h * -scale).astype(BF16)


def diag_mask(half, size):
    rows = lax.broadcasted_iota(jnp.int32, (half, size), 0) + lax.axis_index("col") * half
    return lax.broadcasted_iota(jnp.int32, (half, size), 1) == rows


def start_kernel(
    dims, reach_hbm, bounds_hbm, flag_hbm, h_hbm, x_ref, tail_ref, head_ref, part_ref, h_ref, reach_ref, bounds_ref,
    flag_ref, row_sems, sems,
):
    rows, width, half, size = dims
    first_row = lax.axis_index("row") * rows
    total_rows = lax.axis_size("row") * rows
    small = [
        pltpu.make_async_copy(src, dst, sems.at[n])
        for n, (src, dst) in enumerate(((reach_hbm, reach_ref), (bounds_hbm, bounds_ref), (flag_hbm, flag_ref)))
    ]
    large = [pltpu.make_async_copy(h_hbm.at[i], h_ref.at[i], row_sems.at[i]) for i in range(rows)]
    for copy in small + large:
        copy.start()
    on_diag = diag_mask(half, size)
    place = {block: (tail_ref, n) for n, block in enumerate(tail_blocks(rows, width))}
    heads = {block: (head_ref, n) for n, block in enumerate(head_blocks(width))}

    def fold(block):
        return jnp.sum(block.reshape(half // 8, 8, size), axis=0)

    for copy in small:
        copy.wait()
    diag = jnp.zeros((8, size), F32)
    once = jnp.zeros((8, size), F32)
    twice = jnp.zeros((8, size), F32)
    for row in range(rows):
        large[row].wait()
        for d in range(width + 1):
            kept = is_kept(reach_ref, row, d, first_row, total_rows)
            x = start_block(h_ref[row, d], d, kept, bounds_ref, on_diag)
            x_ref[row, d] = x
            for table in (place, heads):
                if (row, d) in table:
                    ref, n = table[row, d]
                    ref[n] = x
            wide = x.astype(F32)
            if d == 0:
                diag = diag + fold(jnp.where(on_diag, wide, 0.0))
                once = once + fold(wide * wide)
            else:
                twice = twice + fold(wide * wide)
    norm = once + 2.0 * twice
    part_ref[...] = jnp.where(flag_ref[0] == 1, norm, 2.0 * diag - norm)


def strips(rows, width):
    out = []
    for j in range(0, rows + width, 2):
        cols = list(range(j, min(j + 2, rows + width)))
        i_lo, i_hi = max(0, j - width), min(rows - 1, cols[-1])
        k_lo = max(0, j - width)
        k_hi = min(rows + width - 1 if j < rows else rows - 1, cols[-1] + width, i_hi + width)
        out.append((cols, i_lo, i_hi, k_lo, k_hi))
    return out


def inner_kernel(dims, reach_ref, flag_ref, mine_ref, other_ref, out_ref, full, left):
    rows, width, half, size = dims
    column = lax.axis_index("col")
    first_row = lax.axis_index("row") * rows
    total_rows = lax.axis_size("row") * rows
    mine = pl.multiple_of(column * half, half)
    other = pl.multiple_of((1 - column) * half, half)
    zero_full = jnp.zeros((size, size), BF16)
    zero_left = jnp.zeros((half, size), BF16)

    def block(n):
        return pl.ds(n * size, size)

    for k in range(rows):
        for d in range(width + 1):
            full[pl.ds(k * size + mine, half), block(k + d)] = mine_ref[k, d]
            full[pl.ds(k * size + other, half), block(k + d)] = other_ref[k, d]
    have_full = {(k, k + d) for k in range(rows) for d in range(width + 1)}
    for j in range(rows):
        for d in range(1, width + 1):
            full[block(j + d), block(j)] = full[block(j), block(j + d)].T
            have_full.add((j + d, j))
    need_full, need_left = set(), set()
    for cols, i_lo, i_hi, k_lo, k_hi in strips(rows, width):
        need_full |= {(k, j) for k in range(k_lo, k_hi + 1) for j in cols}
        need_left |= {(i, k) for i in range(i_lo, i_hi + 1) for k in range(k_lo, k_hi + 1)}
    for k, j in sorted(need_full - have_full):
        full[block(k), block(j)] = zero_full
    for i, k in sorted(need_left):
        if k < i - width or k > i + width:
            piece = zero_left
        elif k >= i:
            piece = mine_ref[i, k - i]
        else:
            piece = full[pl.ds(i * size + mine, half), block(k)]
        left[pl.ds(i * half, half), block(k)] = piece

    sign = jnp.where(flag_ref[0] == 1, 1.0, -1.0)
    twice = jnp.where(flag_ref[0] == 1, 0.0, 2.0)
    for cols, i_lo, i_hi, k_lo, k_hi in strips(rows, width):
        depth = pl.ds(k_lo * size, (k_hi - k_lo + 1) * size)
        square = jnp.dot(
            left[pl.ds(i_lo * half, (i_hi - i_lo + 1) * half), depth],
            full[depth, pl.ds(cols[0] * size, len(cols) * size)],
            preferred_element_type=F32,
        )
        for n, j in enumerate(cols):
            for i in range(max(i_lo, j - width), min(i_hi, j) + 1):
                d = j - i
                kept = is_kept(reach_ref, i, d, first_row, total_rows)
                part = square[(i - i_lo) * half : (i - i_lo + 1) * half, n * size : (n + 1) * size]
                out_ref[i, d] = part * jnp.where(kept, sign, 0.0) + twice * mine_ref[i, d].astype(F32)


def fetch(base_ref, held, jobs, sems):
    copies = []
    for n, (row, d, count, at) in enumerate(jobs):
        copies.append(pltpu.make_async_copy(base_ref.at[row, pl.ds(d, count)], held.at[pl.ds(at, count)], sems.at[n]))
        copies[-1].start()
    return copies


def finish(dims, reach_ref, flag_ref, square, from_row, from_col, copies, jobs, held, out_ref, sems):
    rows, width, half, size = dims
    first_row = lax.axis_index("row") * rows
    total_rows = lax.axis_size("row") * rows
    sign = jnp.where(flag_ref[0] == 1, 1.0, -1.0)
    backs = []
    for n, (row, d, count, at) in enumerate(jobs):
        copies[n].wait()
        for e in range(count):
            i, j = row - from_row, row + d + e - from_col
            kept = is_kept(reach_ref, row, d + e, first_row, total_rows)
            part = square[i * half : (i + 1) * half, j * size : (j + 1) * size]
            held[at + e] = held[at + e] + part * jnp.where(kept, sign, 0.0)
        copy = pltpu.make_async_copy(held.at[pl.ds(at, count)], out_ref.at[row, pl.ds(d, count)], sems.at[n])
        copy.start()
        backs.append(copy)
    for copy in backs:
        copy.wait()


def halves(dims):
    half = dims[2]
    column = lax.axis_index("col")
    return pl.multiple_of(column * half, half), pl.multiple_of((1 - column) * half, half)


def above_kernel(
    dims, reach_ref, flag_ref, mine_ref, other_ref, base_ref, out_ref, above, above_t, left, held, in_sems, out_sems
):
    rows, width, half, size = dims
    mine, other = halves(dims)
    jobs = runs(head_blocks(width))
    copies = fetch(base_ref, held, jobs, in_sems)

    def block(n):
        return pl.ds(n * size, size)

    have = set()
    for n, (row, d) in enumerate(tail_blocks(rows, width)):
        k, j = row - rows + width, row + d - rows
        above[pl.ds(k * size + mine, half), block(j)] = mine_ref[n]
        above[pl.ds(k * size + other, half), block(j)] = other_ref[n]
        have.add((k, j))
    for k in range(width):
        for j in range(width):
            if (k, j) in have:
                above_t[block(j), block(k)] = above[block(k), block(j)].T
                left[pl.ds(j * half, half), block(k)] = above_t[pl.ds(j * size + mine, half), block(k)]
            else:
                above[block(k), block(j)] = jnp.zeros((size, size), BF16)
                left[pl.ds(j * half, half), block(k)] = jnp.zeros((half, size), BF16)
    square = jnp.dot(left[...], above[...], preferred_element_type=F32)
    finish(dims, reach_ref, flag_ref, square, 0, 0, copies, jobs, held, out_ref, out_sems)


def below_kernel(
    dims, reach_ref, flag_ref, mine_ref, other_ref, own_tail, base_ref, out_ref, below, left, held, in_sems, out_sems
):
    rows, width, half, size = dims
    mine, other = halves(dims)
    jobs = runs(tail_blocks(rows, width))
    copies = fetch(base_ref, held, jobs, in_sems)

    def block(n):
        return pl.ds(n * size, size)

    have = set()
    for n, (row, d) in enumerate(tail_blocks(rows, width)):
        i, k = row - rows + width, row + d - rows
        left[pl.ds(i * half, half), block(k)] = own_tail[n]
        have.add((i, k))
    for i in range(width):
        for k in range(width):
            if (i, k) not in have:
                left[pl.ds(i * half, half), block(k)] = jnp.zeros((half, size), BF16)
    for n, (k, d) in enumerate(head_blocks(width)):
        below[pl.ds(k * size + mine, half), block(k + d)] = mine_ref[n]
        below[pl.ds(k * size + other, half), block(k + d)] = other_ref[n]
        if d:
            below[block(k + d), block(k)] = below[block(k), block(k + d)].T
    square = jnp.dot(left[...], below[...], preferred_element_type=F32)
    finish(dims, reach_ref, flag_ref, square, rows - width, rows, copies, jobs, held, out_ref, out_sems)


def per_device(hamiltonian, bounds, block_reach, branch_flags):
    rows, offsets, half, size = hamiltonian.shape
    width = offsets - 1
    dims = (rows, width, half, size)
    halo = len(head_blocks(width))
    count = lax.axis_size("row")
    down = [(i, i + 1) for i in range(count - 1)]
    up = [(i + 1, i) for i in range(count - 1)]
    swap = [(0, 1), (1, 0)]
    packed = jax.ShapeDtypeStruct((halo, half, size), BF16)
    whole = jax.ShapeDtypeStruct(hamiltonian.shape, F32)

    current, tail, head, part = pl.pallas_call(
        functools.partial(start_kernel, dims),
        out_shape=(
            jax.ShapeDtypeStruct(hamiltonian.shape, BF16), packed, packed, jax.ShapeDtypeStruct((8, size), F32),
        ),
        in_specs=[HBM, HBM, HBM, HBM],
        out_specs=(VMEM, VMEM, VMEM, VMEM),
        scratch_shapes=[
            pltpu.VMEM(hamiltonian.shape, F32),
            pltpu.SMEM(block_reach.shape, jnp.int32),
            pltpu.SMEM(bounds.shape, F32),
            pltpu.SMEM(branch_flags.shape, jnp.int32),
            pltpu.SemaphoreType.DMA((rows,)),
            pltpu.SemaphoreType.DMA((3,)),
        ],
        compiler_params=pltpu.CompilerParams(vmem_limit_bytes=58 * MIB),
        cost_estimate=SMALL,
        name="start",
    )(block_reach, bounds, branch_flags, hamiltonian)
    swapped = lax.ppermute(current, "col", swap)
    below_mine = lax.ppermute(head, "row", up)
    above_mine = lax.ppermute(tail, "row", down)
    parts = lax.all_gather(part, ("row", "col"))

    base = pl.pallas_call(
        functools.partial(inner_kernel, dims),
        out_shape=whole,
        in_specs=[SMEM, SMEM, VMEM, VMEM],
        out_specs=VMEM,
        scratch_shapes=[
            pltpu.VMEM(((rows + width) * size, (rows + width) * size), BF16),
            pltpu.VMEM((rows * half, (rows + width) * size), BF16),
        ],
        compiler_params=pltpu.CompilerParams(vmem_limit_bytes=40 * MIB),
        cost_estimate=SMALL,
        name="inner",
    )(block_reach, branch_flags, current, swapped)

    square = pltpu.VMEM((width * size, width * size), BF16)
    strip = pltpu.VMEM((width * half, width * size), BF16)
    rest = [
        pltpu.VMEM((halo, half, size), F32),
        pltpu.SemaphoreType.DMA((width,)),
        pltpu.SemaphoreType.DMA((width,)),
    ]
    params = pltpu.CompilerParams(vmem_limit_bytes=16 * MIB)
    base, below_mine = lax.optimization_barrier((base, below_mine))
    below_other = lax.ppermute(below_mine, "col", swap)
    base = pl.pallas_call(
        functools.partial(below_kernel, dims),
        out_shape=whole,
        in_specs=[SMEM, SMEM, VMEM, VMEM, VMEM, ANY],
        out_specs=ANY,
        input_output_aliases={5: 0},
        scratch_shapes=[square, strip] + rest,
        compiler_params=params,
        cost_estimate=SMALL,
        name="below",
    )(block_reach, branch_flags, below_mine, below_other, tail, base)
    base, above_mine = lax.optimization_barrier((base, above_mine))
    above_other = lax.ppermute(above_mine, "col", swap)
    density = pl.pallas_call(
        functools.partial(above_kernel, dims),
        out_shape=whole,
        in_specs=[SMEM, SMEM, VMEM, VMEM, ANY],
        out_specs=ANY,
        input_output_aliases={4: 0},
        scratch_shapes=[square, square, strip] + rest,
        compiler_params=params,
        cost_estimate=SMALL,
        name="above",
    )(block_reach, branch_flags, above_mine, above_other, base)
    occupancy = jnp.sum(parts) / (count * rows * size)
    return density, occupancy.reshape(1)


def solution(mesh):
    placed = (
        P(("groups", "row"), None, "col", None),
        P("groups"),
        P(("groups", "row")),
        P("groups"),
    )
    return jax.shard_map(
        per_device,
        mesh=mesh,
        in_specs=placed,
        out_specs=(P(("groups", "row"), None, "col", None), P("groups")),
        check_vma=False,
    )
```

```python
import functools

import jax
import jax.numpy as jnp
from jax import lax
from jax.experimental import pallas as pl
from jax.experimental.pallas import tpu as pltpu
from jax.sharding import PartitionSpec as P

SMEM = pl.BlockSpec(memory_space=pltpu.SMEM)
VMEM = pl.BlockSpec(memory_space=pltpu.VMEM)
ANY = pl.BlockSpec(memory_space=pl.ANY)
HBM = pl.BlockSpec(memory_space=pltpu.HBM)
F32 = jnp.float32
BF16 = jnp.bfloat16
MIB = 1 << 20
SMALL = pl.CostEstimate(flops=1, bytes_accessed=1, transcendentals=0)


def tail_blocks(rows, width):
    return [(rows - m, d) for m in range(1, width + 1) for d in range(m, width + 1)]


def head_blocks(width):
    return [(m, d) for m in range(width) for d in range(width - m)]


def runs(blocks):
    out = []
    for place, (row, d) in enumerate(blocks):
        if out and out[-1][0] == row:
            out[-1][2] += 1
        else:
            out.append([row, d, 1, place])
    return out


def is_kept(reach_ref, row, d, first_row, total_rows):
    return (d <= reach_ref[row]) & (first_row + row + d < total_rows)


def start_block(h, d, kept, bounds_ref, on_diag):
    high = bounds_ref[1]
    scale = jnp.where(kept, 1.0, 0.0) / (high + bounds_ref[0])
    if d == 0:
        return ((jnp.where(on_diag, high, 0.0) - h) * scale).astype(BF16)
    return (h * -scale).astype(BF16)


def diag_mask(half, size):
    rows = lax.broadcasted_iota(jnp.int32, (half, size), 0) + lax.axis_index("col") * half
    return lax.broadcasted_iota(jnp.int32, (half, size), 1) == rows


def start_kernel(
    dims, reach_hbm, bounds_hbm, flag_hbm, h_hbm, x_hbm, tail_hbm, head_hbm, part_ref, h_ref, x_ref, tail_ref, head_ref,
    reach_ref, bounds_ref, flag_ref, in_sems, small_sems, x_sems, halo_sems,
):
    rows, width, half, size = dims
    first_row = lax.axis_index("row") * rows
    total_rows = lax.axis_size("row") * rows
    small = [
        pltpu.make_async_copy(src, dst, small_sems.at[n])
        for n, (src, dst) in enumerate(((reach_hbm, reach_ref), (bounds_hbm, bounds_ref), (flag_hbm, flag_ref)))
    ]
    large = [pltpu.make_async_copy(h_hbm.at[i], h_ref.at[i], in_sems.at[i]) for i in range(rows)]
    for copy in small + large:
        copy.start()
    on_diag = diag_mask(half, size)
    halos = ((head_ref, head_hbm, head_blocks(width)), (tail_ref, tail_hbm, tail_blocks(rows, width)))

    def fold(block):
        return jnp.sum(block.reshape(half // 8, 8, size), axis=0)

    for copy in small:
        copy.wait()
    diag = jnp.zeros((8, size), F32)
    once = jnp.zeros((8, size), F32)
    twice = jnp.zeros((8, size), F32)
    out = []
    for row in range(rows):
        large[row].wait()
        for d in range(width + 1):
            kept = is_kept(reach_ref, row, d, first_row, total_rows)
            x = start_block(h_ref[row, d], d, kept, bounds_ref, on_diag)
            x_ref[row, d] = x
            for ref, _, blocks in halos:
                if (row, d) in blocks:
                    ref[blocks.index((row, d))] = x
            wide = x.astype(F32)
            if d == 0:
                diag = diag + fold(jnp.where(on_diag, wide, 0.0))
                once = once + fold(wide * wide)
            else:
                twice = twice + fold(wide * wide)
        out.append(pltpu.make_async_copy(x_ref.at[row], x_hbm.at[row], x_sems.at[row]))
        out[-1].start()
        for n, (ref, hbm, blocks) in enumerate(halos):
            for at, _, count, place in runs(blocks):
                if at == row:
                    piece = pl.ds(place, count)
                    out.append(pltpu.make_async_copy(ref.at[piece], hbm.at[piece], halo_sems.at[n, place]))
                    out[-1].start()
    norm = once + 2.0 * twice
    part_ref[...] = jnp.where(flag_ref[0] == 1, norm, 2.0 * diag - norm)
    for copy in out:
        copy.wait()


def strips(rows, width):
    out = []
    for j in range(0, rows + width, 2):
        cols = list(range(j, min(j + 2, rows + width)))
        i_lo, i_hi = max(0, j - width), min(rows - 1, cols[-1])
        k_lo = max(0, j - width)
        k_hi = min(rows + width - 1 if j < rows else rows - 1, cols[-1] + width, i_hi + width)
        out.append((cols, i_lo, i_hi, k_lo, k_hi))
    return out


def inner_kernel(dims, reach_ref, flag_ref, mine_ref, other_ref, part_ref, got_ref, out_ref, sum_ref, full, left):
    sum_ref[...] = part_ref[...] + got_ref[...]
    rows, width, half, size = dims
    column = lax.axis_index("col")
    first_row = lax.axis_index("row") * rows
    total_rows = lax.axis_size("row") * rows
    mine = pl.multiple_of(column * half, half)
    other = pl.multiple_of((1 - column) * half, half)
    zero_full = jnp.zeros((size, size), BF16)
    zero_left = jnp.zeros((half, size), BF16)

    def block(n):
        return pl.ds(n * size, size)

    for k in range(rows):
        for d in range(width + 1):
            full[pl.ds(k * size + mine, half), block(k + d)] = mine_ref[k, d]
            full[pl.ds(k * size + other, half), block(k + d)] = other_ref[k, d]
    have_full = {(k, k + d) for k in range(rows) for d in range(width + 1)}
    for j in range(rows):
        for d in range(1, width + 1):
            full[block(j + d), block(j)] = full[block(j), block(j + d)].T
            have_full.add((j + d, j))
    need_full, need_left = set(), set()
    for cols, i_lo, i_hi, k_lo, k_hi in strips(rows, width):
        need_full |= {(k, j) for k in range(k_lo, k_hi + 1) for j in cols}
        need_left |= {(i, k) for i in range(i_lo, i_hi + 1) for k in range(k_lo, k_hi + 1)}
    for k, j in sorted(need_full - have_full):
        full[block(k), block(j)] = zero_full
    for i, k in sorted(need_left):
        if k < i - width or k > i + width:
            piece = zero_left
        elif k >= i:
            piece = mine_ref[i, k - i]
        else:
            piece = full[pl.ds(i * size + mine, half), block(k)]
        left[pl.ds(i * half, half), block(k)] = piece

    sign = jnp.where(flag_ref[0] == 1, 1.0, -1.0)
    twice = jnp.where(flag_ref[0] == 1, 0.0, 2.0)
    for cols, i_lo, i_hi, k_lo, k_hi in strips(rows, width):
        depth = pl.ds(k_lo * size, (k_hi - k_lo + 1) * size)
        square = jnp.dot(
            left[pl.ds(i_lo * half, (i_hi - i_lo + 1) * half), depth],
            full[depth, pl.ds(cols[0] * size, len(cols) * size)],
            preferred_element_type=F32,
        )
        for n, j in enumerate(cols):
            for i in range(max(i_lo, j - width), min(i_hi, j) + 1):
                d = j - i
                kept = is_kept(reach_ref, i, d, first_row, total_rows)
                part = square[(i - i_lo) * half : (i - i_lo + 1) * half, n * size : (n + 1) * size]
                out_ref[i, d] = part * jnp.where(kept, sign, 0.0) + twice * mine_ref[i, d].astype(F32)


def halo_kernel(
    dims, reach_ref, flag_ref, above_mine, above_other, below_mine, below_other, own_tail, base_ref, out_ref,
    above, above_t, above_left, below, tail_left, held, in_sems, out_sems,
):
    rows, width, half, size = dims
    column = lax.axis_index("col")
    first_row = lax.axis_index("row") * rows
    total_rows = lax.axis_size("row") * rows
    mine = pl.multiple_of(column * half, half)
    other = pl.multiple_of((1 - column) * half, half)
    tails, heads = tail_blocks(rows, width), head_blocks(width)

    copies = []
    jobs = [(run, run[3]) for run in runs(heads)] + [(run, len(heads) + run[3]) for run in runs(tails)]
    for n, ((row, d, count, _), at) in enumerate(jobs):
        copy = pltpu.make_async_copy(base_ref.at[row, pl.ds(d, count)], held.at[pl.ds(at, count)], in_sems.at[n])
        copy.start()
        copies.append(copy)

    def block(n):
        return pl.ds(n * size, size)

    zero_full = jnp.zeros((size, size), BF16)
    zero_left = jnp.zeros((half, size), BF16)
    have = set()
    for n, (row, d) in enumerate(tails):
        k, j = row - rows + width, row + d - rows
        above[pl.ds(k * size + mine, half), block(j)] = above_mine[n]
        above[pl.ds(k * size + other, half), block(j)] = above_other[n]
        tail_left[pl.ds(k * half, half), block(j)] = own_tail[n]
        have.add((k, j))
    for k in range(width):
        for j in range(width):
            if (k, j) not in have:
                above[block(k), block(j)] = zero_full
                above_left[pl.ds(j * half, half), block(k)] = zero_left
                tail_left[pl.ds(k * half, half), block(j)] = zero_left
    for k, j in sorted(have):
        above_t[block(j), block(k)] = above[block(k), block(j)].T
        above_left[pl.ds(j * half, half), block(k)] = above_t[pl.ds(j * size + mine, half), block(k)]
    for n, (k, d) in enumerate(heads):
        below[pl.ds(k * size + mine, half), block(k + d)] = below_mine[n]
        below[pl.ds(k * size + other, half), block(k + d)] = below_other[n]
    for k, d in heads:
        if d:
            below[block(k + d), block(k)] = below[block(k), block(k + d)].T
    first = jnp.dot(above_left[...], above[...], preferred_element_type=F32)
    second = jnp.dot(tail_left[...], below[...], preferred_element_type=F32)

    sign = jnp.where(flag_ref[0] == 1, 1.0, -1.0)
    backs = []
    for n, ((row, d, count, _), at) in enumerate(jobs):
        copies[n].wait()
        for e in range(count):
            if n < len(runs(heads)):
                i, j, square = row, row + d + e, first
            else:
                i, j, square = row - rows + width, row + d + e - rows, second
            kept = is_kept(reach_ref, row, d + e, first_row, total_rows)
            part = square[i * half : (i + 1) * half, j * size : (j + 1) * size]
            held[at + e] = held[at + e] + part * jnp.where(kept, sign, 0.0)
        copy = pltpu.make_async_copy(held.at[pl.ds(at, count)], out_ref.at[row, pl.ds(d, count)], out_sems.at[n])
        copy.start()
        backs.append(copy)
    for copy in backs:
        copy.wait()


def per_device(hamiltonian, bounds, block_reach, branch_flags):
    rows, offsets, half, size = hamiltonian.shape
    width = offsets - 1
    dims = (rows, width, half, size)
    halo = len(head_blocks(width))
    count = lax.axis_size("row")
    down = [(i, i + 1) for i in range(count - 1)]
    up = [(i + 1, i) for i in range(count - 1)]
    swap = [(0, 1), (1, 0)]
    packed = jax.ShapeDtypeStruct((halo, half, size), BF16)
    whole = jax.ShapeDtypeStruct(hamiltonian.shape, F32)

    current, tail, head, part = pl.pallas_call(
        functools.partial(start_kernel, dims),
        out_shape=(
            jax.ShapeDtypeStruct(hamiltonian.shape, BF16), packed, packed, jax.ShapeDtypeStruct((8, size), F32),
        ),
        in_specs=[HBM, HBM, HBM, HBM],
        out_specs=(HBM, HBM, HBM, VMEM),
        scratch_shapes=[
            pltpu.VMEM(hamiltonian.shape, F32),
            pltpu.VMEM(hamiltonian.shape, BF16),
            pltpu.VMEM((halo, half, size), BF16),
            pltpu.VMEM((halo, half, size), BF16),
            pltpu.SMEM(block_reach.shape, jnp.int32),
            pltpu.SMEM(bounds.shape, F32),
            pltpu.SMEM(branch_flags.shape, jnp.int32),
            pltpu.SemaphoreType.DMA((rows,)),
            pltpu.SemaphoreType.DMA((3,)),
            pltpu.SemaphoreType.DMA((rows,)),
            pltpu.SemaphoreType.DMA((2, halo)),
        ],
        compiler_params=pltpu.CompilerParams(vmem_limit_bytes=58 * MIB),
        cost_estimate=SMALL,
        name="start",
    )(block_reach, bounds, branch_flags, hamiltonian)
    swapped = lax.ppermute(current, "col", swap)
    got = lax.ppermute(part, "col", swap)
    below_mine = lax.ppermute(head, "row", up)
    above_mine = lax.ppermute(tail, "row", down)

    base, part = pl.pallas_call(
        functools.partial(inner_kernel, dims),
        out_shape=(whole, jax.ShapeDtypeStruct((8, size), F32)),
        in_specs=[SMEM, SMEM, VMEM, VMEM, VMEM, VMEM],
        out_specs=(VMEM, VMEM),
        scratch_shapes=[
            pltpu.VMEM(((rows + width) * size, (rows + width) * size), BF16),
            pltpu.VMEM((rows * half, (rows + width) * size), BF16),
        ],
        compiler_params=pltpu.CompilerParams(vmem_limit_bytes=58 * MIB),
        cost_estimate=SMALL,
        name="inner",
    )(block_reach, branch_flags, current, swapped, part, got)

    far = count
    while far > 2:
        far //= 2
        part = part + lax.ppermute(part, "row", [(i, i ^ far) for i in range(count)])

    base, below_mine, above_mine, part = lax.optimization_barrier((base, below_mine, above_mine, part))
    below_other = lax.ppermute(below_mine, "col", swap)
    above_other = lax.ppermute(above_mine, "col", swap)
    part = part + lax.ppermute(part, "row", [(i, i ^ 1) for i in range(count)])
    density = pl.pallas_call(
        functools.partial(halo_kernel, dims),
        out_shape=whole,
        in_specs=[SMEM, SMEM, VMEM, VMEM, VMEM, VMEM, VMEM, ANY],
        out_specs=ANY,
        input_output_aliases={7: 0},
        scratch_shapes=[
            pltpu.VMEM((width * size, width * size), BF16),
            pltpu.VMEM((width * size, width * size), BF16),
            pltpu.VMEM((width * half, width * size), BF16),
            pltpu.VMEM((width * size, width * size), BF16),
            pltpu.VMEM((width * half, width * size), BF16),
            pltpu.VMEM((2 * halo, half, size), F32),
            pltpu.SemaphoreType.DMA((2 * width,)),
            pltpu.SemaphoreType.DMA((2 * width,)),
        ],
        compiler_params=pltpu.CompilerParams(vmem_limit_bytes=24 * MIB),
        cost_estimate=SMALL,
        name="halo",
    )(block_reach, branch_flags, above_mine, above_other, below_mine, below_other, tail, base)
    occupancy = jnp.sum(part) / (count * rows * size)
    return density, occupancy.reshape(1)


def solution(mesh):
    placed = (
        P(("groups", "row"), None, "col", None),
        P("groups"),
        P(("groups", "row")),
        P("groups"),
    )
    return jax.shard_map(
        per_device,
        mesh=mesh,
        in_specs=placed,
        out_specs=(P(("groups", "row"), None, "col", None), P("groups")),
        check_vma=False,
    )
```

```python
import functools

import jax
import jax.numpy as jnp
from jax import lax
from jax.experimental import pallas as pl
from jax.experimental.pallas import tpu as pltpu
from jax.sharding import PartitionSpec as P

SMEM = pl.BlockSpec(memory_space=pltpu.SMEM)
VMEM = pl.BlockSpec(memory_space=pltpu.VMEM)
ANY = pl.BlockSpec(memory_space=pl.ANY)
HBM = pl.BlockSpec(memory_space=pltpu.HBM)
F32 = jnp.float32
BF16 = jnp.bfloat16
MIB = 1 << 20
LINES = 16
SMALL = pl.CostEstimate(flops=1, bytes_accessed=1, transcendentals=0)


def tail_blocks(rows, width):
    return [(rows - m, d) for m in range(1, width + 1) for d in range(m, width + 1)]


def head_blocks(width):
    return [(m, d) for m in range(width) for d in range(width - m)]


def runs(blocks):
    out = []
    for place, (row, d) in enumerate(blocks):
        if out and out[-1][0] == row:
            out[-1][2] += 1
        else:
            out.append([row, d, 1, place])
    return out


def is_kept(reach_ref, row, d, first_row, total_rows):
    return (d <= reach_ref[row]) & (first_row + row + d < total_rows)


def start_block(h, d, kept, bounds_ref, on_diag):
    high = bounds_ref[1]
    scale = jnp.where(kept, 1.0, 0.0) / (high + bounds_ref[0])
    if d == 0:
        return ((jnp.where(on_diag, high, 0.0) - h) * scale).astype(BF16)
    return (h * -scale).astype(BF16)


def diag_mask(half, size):
    rows = lax.broadcasted_iota(jnp.int32, (half, size), 0) + lax.axis_index("col") * half
    return lax.broadcasted_iota(jnp.int32, (half, size), 1) == rows


def start_kernel(
    dims, reach_hbm, bounds_hbm, flag_hbm, h_hbm, x_ref, near_ref, far_ref, part_ref, h_ref, reach_ref, bounds_ref,
    flag_ref, in_sems, small_sems,
):
    rows, width, half, size = dims
    first_row = lax.axis_index("row") * rows
    total_rows = lax.axis_size("row") * rows
    small = [
        pltpu.make_async_copy(src, dst, small_sems.at[n])
        for n, (src, dst) in enumerate(((reach_hbm, reach_ref), (bounds_hbm, bounds_ref), (flag_hbm, flag_ref)))
    ]
    large = [pltpu.make_async_copy(h_hbm.at[i], h_ref.at[i], in_sems.at[i]) for i in range(rows)]
    for copy in small + large:
        copy.start()
    on_diag = diag_mask(half, size)

    def fold(block):
        return jnp.sum(block.reshape(half // LINES, LINES, size), axis=0)

    for copy in small:
        copy.wait()
    diag = jnp.zeros((LINES, size), F32)
    once = jnp.zeros((LINES, size), F32)
    twice = jnp.zeros((LINES, size), F32)
    for row in range(rows):
        large[row].wait()
        for d in range(width + 1):
            kept = is_kept(reach_ref, row, d, first_row, total_rows)
            x = start_block(h_ref[row, d], d, kept, bounds_ref, on_diag)
            x_ref[row, d] = x
            wide = x.astype(F32)
            if d == 0:
                diag = diag + fold(jnp.where(on_diag, wide, 0.0))
                once = once + fold(wide * wide)
            else:
                twice = twice + fold(wide * wide)
    norm = once + 2.0 * twice
    part = jnp.where(flag_ref[0] == 1, norm, 2.0 * diag - norm)
    part_ref[...] = part

    tails, heads = tail_blocks(rows, width), head_blocks(width)
    for parity, near, far in ((0, tails, heads), (1, heads, tails)):

        @pl.when(lax.axis_index("row") % 2 == parity)
        def _(near=near, far=far):
            for ref, blocks in ((near_ref, near), (far_ref, far)):
                for n, (row, d) in enumerate(blocks):
                    ref[n] = x_ref[row, d]

    for n in range(half // LINES):
        term = part.astype(BF16) if n < 3 else jnp.zeros((LINES, size), BF16)
        near_ref[len(heads), pl.ds(n * LINES, LINES)] = term
        part = part - term.astype(F32)


def strips(rows, width):
    out = []
    for j in range(0, rows + width, 2):
        cols = list(range(j, min(j + 2, rows + width)))
        i_lo, i_hi = max(0, j - width), min(rows - 1, cols[-1])
        k_lo = max(0, j - width)
        k_hi = min(rows + width - 1 if j < rows else rows - 1, cols[-1] + width, i_hi + width)
        out.append((cols, i_lo, i_hi, k_lo, k_hi))
    return out


def inner_kernel(dims, reach_ref, flag_ref, mine_ref, other_ref, out_hbm, out_ref, full, left, sems):
    rows, width, half, size = dims
    column = lax.axis_index("col")
    first_row = lax.axis_index("row") * rows
    total_rows = lax.axis_size("row") * rows
    mine = pl.multiple_of(column * half, half)
    other = pl.multiple_of((1 - column) * half, half)
    zero_full = jnp.zeros((size, size), BF16)
    zero_left = jnp.zeros((half, size), BF16)

    def block(n):
        return pl.ds(n * size, size)

    for k in range(rows):
        for d in range(width + 1):
            full[pl.ds(k * size + mine, half), block(k + d)] = mine_ref[k, d]
            full[pl.ds(k * size + other, half), block(k + d)] = other_ref[k, d]
    have_full = {(k, k + d) for k in range(rows) for d in range(width + 1)}
    for j in range(rows):
        for d in range(1, width + 1):
            full[block(j + d), block(j)] = full[block(j), block(j + d)].T
            have_full.add((j + d, j))
    need_full, need_left = set(), set()
    for cols, i_lo, i_hi, k_lo, k_hi in strips(rows, width):
        need_full |= {(k, j) for k in range(k_lo, k_hi + 1) for j in cols}
        need_left |= {(i, k) for i in range(i_lo, i_hi + 1) for k in range(k_lo, k_hi + 1)}
    for k, j in sorted(need_full - have_full):
        full[block(k), block(j)] = zero_full
    for i, k in sorted(need_left):
        if k < i - width or k > i + width:
            piece = zero_left
        elif k >= i:
            piece = mine_ref[i, k - i]
        else:
            piece = full[pl.ds(i * size + mine, half), block(k)]
        left[pl.ds(i * half, half), block(k)] = piece

    sign = jnp.where(flag_ref[0] == 1, 1.0, -1.0)
    twice = jnp.where(flag_ref[0] == 1, 0.0, 2.0)
    for cols, i_lo, i_hi, k_lo, k_hi in strips(rows, width):
        depth = pl.ds(k_lo * size, (k_hi - k_lo + 1) * size)
        square = jnp.dot(
            left[pl.ds(i_lo * half, (i_hi - i_lo + 1) * half), depth],
            full[depth, pl.ds(cols[0] * size, len(cols) * size)],
            preferred_element_type=F32,
        )
        for n, j in enumerate(cols):
            for i in range(max(i_lo, j - width), min(i_hi, j) + 1):
                d = j - i
                kept = is_kept(reach_ref, i, d, first_row, total_rows)
                part = square[(i - i_lo) * half : (i - i_lo + 1) * half, n * size : (n + 1) * size]
                out_ref[i, d] = part * jnp.where(kept, sign, 0.0) + twice * mine_ref[i, d].astype(F32)
                if d == width:
                    pltpu.make_async_copy(out_ref.at[i], out_hbm.at[i], sems.at[i]).start()
    for i in range(rows):
        pltpu.make_async_copy(out_ref.at[i], out_hbm.at[i], sems.at[i]).wait()


def fetch(base_ref, held, jobs, sems):
    copies = []
    for n, (row, d, count, at) in enumerate(jobs):
        copies.append(pltpu.make_async_copy(base_ref.at[row, pl.ds(d, count)], held.at[pl.ds(at, count)], sems.at[n]))
        copies[-1].start()
    return copies


def finish(dims, reach_ref, flag_ref, square, from_row, from_col, copies, jobs, held, out_ref, sems):
    rows, width, half, size = dims
    first_row = lax.axis_index("row") * rows
    total_rows = lax.axis_size("row") * rows
    sign = jnp.where(flag_ref[0] == 1, 1.0, -1.0)
    backs = []
    for n, (row, d, count, at) in enumerate(jobs):
        copies[n].wait()
        for e in range(count):
            i, j = row - from_row, row + d + e - from_col
            kept = is_kept(reach_ref, row, d + e, first_row, total_rows)
            part = square[i * half : (i + 1) * half, j * size : (j + 1) * size]
            held[at + e] = held[at + e] + part * jnp.where(kept, sign, 0.0)
        copy = pltpu.make_async_copy(held.at[pl.ds(at, count)], out_ref.at[row, pl.ds(d, count)], sems.at[n])
        copy.start()
        backs.append(copy)
    for copy in backs:
        copy.wait()


def halves(dims):
    half = dims[2]
    column = lax.axis_index("col")
    return pl.multiple_of(column * half, half), pl.multiple_of((1 - column) * half, half)


def add_above(dims, reach_ref, flag_ref, mine_ref, other_ref, base_ref, out_ref, whole, turned, left, held, in_sems, out_sems):
    rows, width, half, size = dims
    mine, other = halves(dims)
    jobs = runs(head_blocks(width))
    copies = fetch(base_ref, held, jobs, in_sems)

    def block(n):
        return pl.ds(n * size, size)

    have = set()
    for n, (row, d) in enumerate(tail_blocks(rows, width)):
        k, j = row - rows + width, row + d - rows
        whole[pl.ds(k * size + mine, half), block(j)] = mine_ref[n]
        whole[pl.ds(k * size + other, half), block(j)] = other_ref[n]
        have.add((k, j))
    for k in range(width):
        for j in range(width):
            if (k, j) in have:
                turned[block(j), block(k)] = whole[block(k), block(j)].T
                left[pl.ds(j * half, half), block(k)] = turned[pl.ds(j * size + mine, half), block(k)]
            else:
                whole[block(k), block(j)] = jnp.zeros((size, size), BF16)
                left[pl.ds(j * half, half), block(k)] = jnp.zeros((half, size), BF16)
    square = jnp.dot(left[...], whole[...], preferred_element_type=F32)
    finish(dims, reach_ref, flag_ref, square, 0, 0, copies, jobs, held, out_ref, out_sems)


def add_below(dims, reach_ref, flag_ref, mine_ref, other_ref, sent_ref, base_ref, out_ref, whole, left, held, in_sems, out_sems):
    rows, width, half, size = dims
    mine, other = halves(dims)
    jobs = runs(tail_blocks(rows, width))
    copies = fetch(base_ref, held, jobs, in_sems)

    def block(n):
        return pl.ds(n * size, size)

    have = set()
    for n, (row, d) in enumerate(tail_blocks(rows, width)):
        i, k = row - rows + width, row + d - rows
        left[pl.ds(i * half, half), block(k)] = sent_ref[n]
        have.add((i, k))
    for i in range(width):
        for k in range(width):
            if (i, k) not in have:
                left[pl.ds(i * half, half), block(k)] = jnp.zeros((half, size), BF16)
    for n, (k, d) in enumerate(head_blocks(width)):
        whole[pl.ds(k * size + mine, half), block(k + d)] = mine_ref[n]
        whole[pl.ds(k * size + other, half), block(k + d)] = other_ref[n]
        if d:
            whole[block(k + d), block(k)] = whole[block(k), block(k + d)].T
    square = jnp.dot(left[...], whole[...], preferred_element_type=F32)
    finish(dims, reach_ref, flag_ref, square, rows - width, rows, copies, jobs, held, out_ref, out_sems)


def halo_kernel(
    dims, reach_ref, flag_ref, near_mine, near_other, near_sent, far_mine, far_other, far_sent, trace_ref, got_ref, base_ref,
    out_ref, sum_ref, whole, turned, left, held, whole2, left2, held2, sems,
):
    rows, width, half, size = dims
    sum_ref[...] = jnp.broadcast_to(jnp.sum(trace_ref[...] + got_ref[...]), sum_ref.shape)

    for parity, above, below in (
        (0, (far_mine, far_other), (near_mine, near_other, near_sent)),
        (1, (near_mine, near_other), (far_mine, far_other, far_sent)),
    ):

        @pl.when(lax.axis_index("row") % 2 == parity)
        def _(above=above, below=below):
            add_above(dims, reach_ref, flag_ref, *above, base_ref, out_ref, whole, turned, left, held, sems.at[0], sems.at[1])
            add_below(dims, reach_ref, flag_ref, *below, base_ref, out_ref, whole2, left2, held2, sems.at[2], sems.at[3])


def per_device(hamiltonian, bounds, block_reach, branch_flags):
    rows, offsets, half, size = hamiltonian.shape
    width = offsets - 1
    dims = (rows, width, half, size)
    halo = len(head_blocks(width))
    count = lax.axis_size("row")
    near_pairs = [(i, i ^ 1) for i in range(count)]
    far_pairs = [(i, j) for i in range(count) for j in [((i + 1) ^ 1) - 1] if 0 <= j < count]
    swap = [(0, 1), (1, 0)]
    whole = jax.ShapeDtypeStruct(hamiltonian.shape, F32)

    current, near, far, part = pl.pallas_call(
        functools.partial(start_kernel, dims),
        out_shape=(
            jax.ShapeDtypeStruct(hamiltonian.shape, BF16),
            jax.ShapeDtypeStruct((halo + 1, half, size), BF16),
            jax.ShapeDtypeStruct((halo, half, size), BF16),
            jax.ShapeDtypeStruct((LINES, size), F32),
        ),
        in_specs=[HBM, HBM, HBM, HBM],
        out_specs=(VMEM, VMEM, VMEM, VMEM),
        scratch_shapes=[
            pltpu.VMEM(hamiltonian.shape, F32),
            pltpu.SMEM(block_reach.shape, jnp.int32),
            pltpu.SMEM(bounds.shape, F32),
            pltpu.SMEM(branch_flags.shape, jnp.int32),
            pltpu.SemaphoreType.DMA((rows,)),
            pltpu.SemaphoreType.DMA((3,)),
        ],
        compiler_params=pltpu.CompilerParams(vmem_limit_bytes=58 * MIB),
        cost_estimate=SMALL,
        name="start",
    )(block_reach, bounds, branch_flags, hamiltonian)
    swapped = lax.ppermute(current, "col", swap)
    near_mine = lax.ppermute(near, "row", near_pairs)
    far_mine = lax.ppermute(far, "row", far_pairs)

    base = pl.pallas_call(
        functools.partial(inner_kernel, dims),
        out_shape=whole,
        in_specs=[SMEM, SMEM, VMEM, VMEM],
        out_specs=HBM,
        scratch_shapes=[
            pltpu.VMEM(hamiltonian.shape, F32),
            pltpu.VMEM(((rows + width) * size, (rows + width) * size), BF16),
            pltpu.VMEM((rows * half, (rows + width) * size), BF16),
            pltpu.SemaphoreType.DMA((rows,)),
        ],
        compiler_params=pltpu.CompilerParams(vmem_limit_bytes=24 * MIB),
        cost_estimate=SMALL,
        name="inner",
    )(block_reach, branch_flags, current, swapped)

    base, near_mine = lax.optimization_barrier((base, near_mine))
    terms = near_mine[halo].astype(F32).reshape(half // LINES, LINES, size)
    trace = part + (terms[0] + terms[1] + terms[2])
    far_step = count // 2
    while far_step > 1:
        trace = trace + lax.ppermute(trace, "row", [(i, i ^ far_step) for i in range(count)])
        far_step //= 2

    base, near_mine, far_mine, trace = lax.optimization_barrier((base, near_mine, far_mine, trace))
    near_other = lax.ppermute(near_mine, "col", swap)
    far_other = lax.ppermute(far_mine, "col", swap)
    got = lax.ppermute(trace, "col", swap)
    square = pltpu.VMEM((width * size, width * size), BF16)
    strip = pltpu.VMEM((width * half, width * size), BF16)
    held = pltpu.VMEM((halo, half, size), F32)
    density, total = pl.pallas_call(
        functools.partial(halo_kernel, dims),
        out_shape=(whole, jax.ShapeDtypeStruct((8, size), F32)),
        in_specs=[SMEM, SMEM] + [VMEM] * 8 + [ANY],
        out_specs=(ANY, VMEM),
        input_output_aliases={10: 0},
        scratch_shapes=[square, square, strip, held, square, strip, held, pltpu.SemaphoreType.DMA((4, width))],
        compiler_params=pltpu.CompilerParams(vmem_limit_bytes=24 * MIB),
        cost_estimate=SMALL,
        name="halo",
    )(block_reach, branch_flags, near_mine, near_other, near, far_mine, far_other, far, trace, got, base)
    return density, total[0, :1] / (count * rows * size)


def solution(mesh):
    placed = (
        P(("groups", "row"), None, "col", None),
        P("groups"),
        P(("groups", "row")),
        P("groups"),
    )
    return jax.shard_map(
        per_device,
        mesh=mesh,
        in_specs=placed,
        out_specs=(P(("groups", "row"), None, "col", None), P("groups")),
        check_vma=False,
    )
```

```python
import functools

import jax
import jax.numpy as jnp
from jax import lax
from jax.experimental import pallas as pl
from jax.experimental.pallas import tpu as pltpu
from jax.sharding import PartitionSpec as P

SMEM = pl.BlockSpec(memory_space=pltpu.SMEM)
VMEM = pl.BlockSpec(memory_space=pltpu.VMEM)
ANY = pl.BlockSpec(memory_space=pl.ANY)
HBM = pl.BlockSpec(memory_space=pltpu.HBM)
F32 = jnp.float32
BF16 = jnp.bfloat16
MIB = 1 << 20
LINES = 16
SMALL = pl.CostEstimate(flops=1, bytes_accessed=1, transcendentals=0)


def tail_blocks(rows, width):
    return [(rows - m, d) for m in range(1, width + 1) for d in range(m, width + 1)]


def head_blocks(width):
    return [(m, d) for m in range(width) for d in range(width - m)]


def runs(blocks):
    out = []
    for place, (row, d) in enumerate(blocks):
        if out and out[-1][0] == row:
            out[-1][2] += 1
        else:
            out.append([row, d, 1, place])
    return out


def is_kept(reach_ref, row, d, first_row, total_rows):
    return (d <= reach_ref[row]) & (first_row + row + d < total_rows)


def start_block(h, d, kept, bounds_ref, on_diag):
    high = bounds_ref[1]
    scale = jnp.where(kept, 1.0, 0.0) / (high + bounds_ref[0])
    if d == 0:
        return ((jnp.where(on_diag, high, 0.0) - h) * scale).astype(BF16)
    return (h * -scale).astype(BF16)


def diag_mask(half, size):
    rows = lax.broadcasted_iota(jnp.int32, (half, size), 0) + lax.axis_index("col") * half
    return lax.broadcasted_iota(jnp.int32, (half, size), 1) == rows


def pack_halo(dims, tail_parity, x_ref, out_ref):
    rows, width = dims[:2]
    for parity in (0, 1):

        @pl.when(lax.axis_index("row") % 2 == parity)
        def _(parity=parity):
            blocks = tail_blocks(rows, width) if parity == tail_parity else head_blocks(width)
            for n, (row, d) in enumerate(blocks):
                out_ref[n] = x_ref[row, d]


def start_kernel(
    dims, reach_hbm, bounds_hbm, flag_hbm, h_hbm, x_ref, near_ref, part_ref, h_ref, reach_ref, bounds_ref,
    flag_ref, in_sems, small_sems,
):
    rows, width, half, size = dims
    first_row = lax.axis_index("row") * rows
    total_rows = lax.axis_size("row") * rows
    small = [
        pltpu.make_async_copy(src, dst, small_sems.at[n])
        for n, (src, dst) in enumerate(((reach_hbm, reach_ref), (bounds_hbm, bounds_ref), (flag_hbm, flag_ref)))
    ]
    large = [pltpu.make_async_copy(h_hbm.at[i], h_ref.at[i], in_sems.at[i]) for i in range(rows)]
    for copy in small + large:
        copy.start()
    on_diag = diag_mask(half, size)

    def fold(block):
        return jnp.sum(block.reshape(half // LINES, LINES, size), axis=0)

    for copy in small:
        copy.wait()
    diag = jnp.zeros((LINES, size), F32)
    once = jnp.zeros((LINES, size), F32)
    twice = jnp.zeros((LINES, size), F32)
    for row in range(rows):
        large[row].wait()
        for d in range(width + 1):
            kept = is_kept(reach_ref, row, d, first_row, total_rows)
            x = start_block(h_ref[row, d], d, kept, bounds_ref, on_diag)
            x_ref[row, d] = x
            wide = x.astype(F32)
            if d == 0:
                diag = diag + fold(jnp.where(on_diag, wide, 0.0))
                once = once + fold(wide * wide)
            else:
                twice = twice + fold(wide * wide)
    norm = once + 2.0 * twice
    part = jnp.where(flag_ref[0] == 1, norm, 2.0 * diag - norm)
    part_ref[...] = part

    pack_halo(dims, 0, x_ref, near_ref)
    for n in range(half // LINES):
        term = part.astype(BF16) if n < 3 else jnp.zeros((LINES, size), BF16)
        near_ref[near_ref.shape[0] - 1, pl.ds(n * LINES, LINES)] = term
        part = part - term.astype(F32)


def strips(rows, width):
    out = []
    for j in range(0, rows + width, 2):
        cols = list(range(j, min(j + 2, rows + width)))
        i_lo, i_hi = max(0, j - width), min(rows - 1, cols[-1])
        k_lo = max(0, j - width)
        k_hi = min(rows + width - 1 if j < rows else rows - 1, cols[-1] + width, i_hi + width)
        out.append((cols, i_lo, i_hi, k_lo, k_hi))
    return out


def inner_kernel(dims, reach_ref, flag_ref, mine_ref, other_ref, out_hbm, far_ref, out_ref, full, left, sems):
    pack_halo(dims, 1, mine_ref, far_ref)
    rows, width, half, size = dims
    column = lax.axis_index("col")
    first_row = lax.axis_index("row") * rows
    total_rows = lax.axis_size("row") * rows
    mine = pl.multiple_of(column * half, half)
    other = pl.multiple_of((1 - column) * half, half)
    zero_full = jnp.zeros((size, size), BF16)
    zero_left = jnp.zeros((half, size), BF16)

    def block(n):
        return pl.ds(n * size, size)

    for k in range(rows):
        for d in range(width + 1):
            full[pl.ds(k * size + mine, half), block(k + d)] = mine_ref[k, d]
            full[pl.ds(k * size + other, half), block(k + d)] = other_ref[k, d]
    have_full = {(k, k + d) for k in range(rows) for d in range(width + 1)}
    for j in range(rows):
        for d in range(1, width + 1):
            full[block(j + d), block(j)] = full[block(j), block(j + d)].T
            have_full.add((j + d, j))
    need_full, need_left = set(), set()
    for cols, i_lo, i_hi, k_lo, k_hi in strips(rows, width):
        need_full |= {(k, j) for k in range(k_lo, k_hi + 1) for j in cols}
        need_left |= {(i, k) for i in range(i_lo, i_hi + 1) for k in range(k_lo, k_hi + 1)}
    for k, j in sorted(need_full - have_full):
        full[block(k), block(j)] = zero_full
    for i, k in sorted(need_left):
        if k < i - width or k > i + width:
            piece = zero_left
        elif k >= i:
            piece = mine_ref[i, k - i]
        else:
            piece = full[pl.ds(i * size + mine, half), block(k)]
        left[pl.ds(i * half, half), block(k)] = piece

    sign = jnp.where(flag_ref[0] == 1, 1.0, -1.0)
    twice = jnp.where(flag_ref[0] == 1, 0.0, 2.0)
    for cols, i_lo, i_hi, k_lo, k_hi in strips(rows, width):
        depth = pl.ds(k_lo * size, (k_hi - k_lo + 1) * size)
        square = jnp.dot(
            left[pl.ds(i_lo * half, (i_hi - i_lo + 1) * half), depth],
            full[depth, pl.ds(cols[0] * size, len(cols) * size)],
            preferred_element_type=F32,
        )
        for n, j in enumerate(cols):
            for i in range(max(i_lo, j - width), min(i_hi, j) + 1):
                d = j - i
                kept = is_kept(reach_ref, i, d, first_row, total_rows)
                part = square[(i - i_lo) * half : (i - i_lo + 1) * half, n * size : (n + 1) * size]
                out_ref[i, d] = part * jnp.where(kept, sign, 0.0) + twice * mine_ref[i, d].astype(F32)
                if d == width:
                    pltpu.make_async_copy(out_ref.at[i], out_hbm.at[i], sems.at[i]).start()
    for i in range(rows):
        pltpu.make_async_copy(out_ref.at[i], out_hbm.at[i], sems.at[i]).wait()


def fetch(base_ref, held, jobs, sems):
    copies = []
    for n, (row, d, count, at) in enumerate(jobs):
        copies.append(pltpu.make_async_copy(base_ref.at[row, pl.ds(d, count)], held.at[pl.ds(at, count)], sems.at[n]))
        copies[-1].start()
    return copies


def finish(dims, reach_ref, flag_ref, square, from_row, from_col, copies, jobs, held, out_ref, sems):
    rows, width, half, size = dims
    first_row = lax.axis_index("row") * rows
    total_rows = lax.axis_size("row") * rows
    sign = jnp.where(flag_ref[0] == 1, 1.0, -1.0)
    backs = []
    for n, (row, d, count, at) in enumerate(jobs):
        copies[n].wait()
        for e in range(count):
            i, j = row - from_row, row + d + e - from_col
            kept = is_kept(reach_ref, row, d + e, first_row, total_rows)
            part = square[i * half : (i + 1) * half, j * size : (j + 1) * size]
            held[at + e] = held[at + e] + part * jnp.where(kept, sign, 0.0)
        copy = pltpu.make_async_copy(held.at[pl.ds(at, count)], out_ref.at[row, pl.ds(d, count)], sems.at[n])
        copy.start()
        backs.append(copy)
    for copy in backs:
        copy.wait()


def halves(dims):
    half = dims[2]
    column = lax.axis_index("col")
    return pl.multiple_of(column * half, half), pl.multiple_of((1 - column) * half, half)


def add_above(dims, reach_ref, flag_ref, mine_ref, other_ref, base_ref, out_ref, whole, turned, left, held, in_sems, out_sems):
    rows, width, half, size = dims
    mine, other = halves(dims)
    jobs = runs(head_blocks(width))
    copies = fetch(base_ref, held, jobs, in_sems)

    def block(n):
        return pl.ds(n * size, size)

    have = set()
    for n, (row, d) in enumerate(tail_blocks(rows, width)):
        k, j = row - rows + width, row + d - rows
        whole[pl.ds(k * size + mine, half), block(j)] = mine_ref[n]
        whole[pl.ds(k * size + other, half), block(j)] = other_ref[n]
        have.add((k, j))
    for k in range(width):
        for j in range(width):
            if (k, j) in have:
                turned[block(j), block(k)] = whole[block(k), block(j)].T
                left[pl.ds(j * half, half), block(k)] = turned[pl.ds(j * size + mine, half), block(k)]
            else:
                whole[block(k), block(j)] = jnp.zeros((size, size), BF16)
                left[pl.ds(j * half, half), block(k)] = jnp.zeros((half, size), BF16)
    square = jnp.dot(left[...], whole[...], preferred_element_type=F32)
    finish(dims, reach_ref, flag_ref, square, 0, 0, copies, jobs, held, out_ref, out_sems)


def add_below(dims, reach_ref, flag_ref, mine_ref, other_ref, sent_ref, base_ref, out_ref, whole, left, held, in_sems, out_sems):
    rows, width, half, size = dims
    mine, other = halves(dims)
    jobs = runs(tail_blocks(rows, width))
    copies = fetch(base_ref, held, jobs, in_sems)

    def block(n):
        return pl.ds(n * size, size)

    have = set()
    for n, (row, d) in enumerate(tail_blocks(rows, width)):
        i, k = row - rows + width, row + d - rows
        left[pl.ds(i * half, half), block(k)] = sent_ref[n]
        have.add((i, k))
    for i in range(width):
        for k in range(width):
            if (i, k) not in have:
                left[pl.ds(i * half, half), block(k)] = jnp.zeros((half, size), BF16)
    for n, (k, d) in enumerate(head_blocks(width)):
        whole[pl.ds(k * size + mine, half), block(k + d)] = mine_ref[n]
        whole[pl.ds(k * size + other, half), block(k + d)] = other_ref[n]
        if d:
            whole[block(k + d), block(k)] = whole[block(k), block(k + d)].T
    square = jnp.dot(left[...], whole[...], preferred_element_type=F32)
    finish(dims, reach_ref, flag_ref, square, rows - width, rows, copies, jobs, held, out_ref, out_sems)


def halo_kernel(
    dims, above_parity, reach_ref, flag_ref, mine_ref, other_ref, sent_ref, trace_ref, got_ref, base_ref, out_ref, sum_ref,
    whole, turned, left, held, sems,
):
    total = jnp.sum(trace_ref[...] + got_ref[...])
    sum_ref[0] = total / (lax.axis_size("row") * dims[0] * dims[3])
    parity = lax.axis_index("row") % 2

    @pl.when(parity == above_parity)
    def _():
        add_above(
            dims, reach_ref, flag_ref, mine_ref, other_ref, base_ref, out_ref, whole, turned, left, held, sems.at[0], sems.at[1]
        )

    @pl.when(parity != above_parity)
    def _():
        add_below(
            dims, reach_ref, flag_ref, mine_ref, other_ref, sent_ref, base_ref, out_ref, whole, left, held, sems.at[0], sems.at[1]
        )


def per_device(hamiltonian, bounds, block_reach, branch_flags):
    rows, offsets, half, size = hamiltonian.shape
    width = offsets - 1
    dims = (rows, width, half, size)
    halo = len(head_blocks(width))
    count = lax.axis_size("row")
    near_pairs = [(i, i ^ 1) for i in range(count)]
    far_pairs = [(i, j) for i in range(count) for j in [((i + 1) ^ 1) - 1] if 0 <= j < count]
    swap = [(0, 1), (1, 0)]
    whole = jax.ShapeDtypeStruct(hamiltonian.shape, F32)

    current, near, part = pl.pallas_call(
        functools.partial(start_kernel, dims),
        out_shape=(
            jax.ShapeDtypeStruct(hamiltonian.shape, BF16),
            jax.ShapeDtypeStruct((halo + 1, half, size), BF16),
            jax.ShapeDtypeStruct((LINES, size), F32),
        ),
        in_specs=[HBM, HBM, HBM, HBM],
        out_specs=(VMEM, VMEM, VMEM),
        scratch_shapes=[
            pltpu.VMEM(hamiltonian.shape, F32),
            pltpu.SMEM(block_reach.shape, jnp.int32),
            pltpu.SMEM(bounds.shape, F32),
            pltpu.SMEM(branch_flags.shape, jnp.int32),
            pltpu.SemaphoreType.DMA((rows,)),
            pltpu.SemaphoreType.DMA((3,)),
        ],
        compiler_params=pltpu.CompilerParams(vmem_limit_bytes=58 * MIB),
        cost_estimate=SMALL,
        name="start",
    )(block_reach, bounds, branch_flags, hamiltonian)
    swapped = lax.ppermute(current, "col", swap)
    got = lax.ppermute(part, "col", swap)
    near_mine = lax.ppermute(near, "row", near_pairs)

    base, far = pl.pallas_call(
        functools.partial(inner_kernel, dims),
        out_shape=(whole, jax.ShapeDtypeStruct((halo, half, size), BF16)),
        in_specs=[SMEM, SMEM, VMEM, VMEM],
        out_specs=(HBM, VMEM),
        scratch_shapes=[
            pltpu.VMEM(hamiltonian.shape, F32),
            pltpu.VMEM(((rows + width) * size, (rows + width) * size), BF16),
            pltpu.VMEM((rows * half, (rows + width) * size), BF16),
            pltpu.SemaphoreType.DMA((rows,)),
        ],
        compiler_params=pltpu.CompilerParams(vmem_limit_bytes=24 * MIB),
        cost_estimate=SMALL,
        name="inner",
    )(block_reach, branch_flags, current, swapped)

    far_mine = lax.ppermute(far, "row", far_pairs)

    def add_halo(above_parity, mine, other, sent, trace, got, base):
        square = pltpu.VMEM((width * size, width * size), BF16)
        return pl.pallas_call(
            functools.partial(halo_kernel, dims, above_parity),
            out_shape=(whole, jax.ShapeDtypeStruct((1,), F32)),
            in_specs=[SMEM, SMEM, VMEM, VMEM, VMEM, VMEM, VMEM, ANY],
            out_specs=(ANY, SMEM),
            input_output_aliases={7: 0},
            scratch_shapes=[
                square, square, pltpu.VMEM((width * half, width * size), BF16), pltpu.VMEM((halo, half, size), F32),
                pltpu.SemaphoreType.DMA((2, width)),
            ],
            compiler_params=pltpu.CompilerParams(vmem_limit_bytes=16 * MIB),
            cost_estimate=SMALL,
            name="halo",
        )(block_reach, branch_flags, mine, other, sent, trace, got, base)

    base, near_mine = lax.optimization_barrier((base, near_mine))
    near_other = lax.ppermute(near_mine, "col", swap)
    terms = (near_mine[halo].astype(F32) + near_other[halo].astype(F32)).reshape(half // LINES, LINES, size)
    trace = part + got + (terms[0] + terms[1] + terms[2])
    got, step = jnp.zeros_like(part), count // 2
    while step > 2:
        got = lax.ppermute(trace, "row", [(i, i ^ step) for i in range(count)])
        step //= 2
        if step > 2:
            trace = trace + got
    base, _ = add_halo(1, near_mine, near_other, near, part, part, base)
    base, got = lax.optimization_barrier((base, got))
    trace = trace + got
    got = lax.ppermute(trace, "row", [(i, i ^ 2) for i in range(count)])

    base, far_mine, trace = lax.optimization_barrier((base, far_mine, trace))
    far_other = lax.ppermute(far_mine, "col", swap)
    return add_halo(0, far_mine, far_other, far, trace, got, base)


def solution(mesh):
    placed = (
        P(("groups", "row"), None, "col", None),
        P("groups"),
        P(("groups", "row")),
        P("groups"),
    )
    return jax.shard_map(
        per_device,
        mesh=mesh,
        in_specs=placed,
        out_specs=(P(("groups", "row"), None, "col", None), P("groups")),
        check_vma=False,
    )
```

```python
import functools

import jax
import jax.numpy as jnp
from jax import lax
from jax.experimental import pallas as pl
from jax.experimental.pallas import tpu as pltpu
from jax.sharding import PartitionSpec as P

SMEM = pl.BlockSpec(memory_space=pltpu.SMEM)
VMEM = pl.BlockSpec(memory_space=pltpu.VMEM)
ANY = pl.BlockSpec(memory_space=pl.ANY)
HBM = pl.BlockSpec(memory_space=pltpu.HBM)
F32 = jnp.float32
BF16 = jnp.bfloat16
MIB = 1 << 20
LINES = 16
CUT = 5
SMALL = pl.CostEstimate(flops=1, bytes_accessed=1, transcendentals=0)


def tail_blocks(rows, width):
    return [(rows - m, d) for m in range(1, width + 1) for d in range(m, width + 1)]


def head_blocks(width):
    return [(m, d) for m in range(width) for d in range(width - m)]


def runs(blocks):
    out = []
    for place, (row, d) in enumerate(blocks):
        if out and out[-1][0] == row:
            out[-1][2] += 1
        else:
            out.append([row, d, 1, place])
    return out


def is_kept(reach_ref, row, d, first_row, total_rows):
    return (d <= reach_ref[row]) & (first_row + row + d < total_rows)


def start_block(h, d, kept, bounds_ref, on_diag):
    high = bounds_ref[1]
    scale = jnp.where(kept, 1.0, 0.0) / (high + bounds_ref[0])
    if d == 0:
        return ((jnp.where(on_diag, high, 0.0) - h) * scale).astype(BF16)
    return (h * -scale).astype(BF16)


def diag_mask(half, size):
    rows = lax.broadcasted_iota(jnp.int32, (half, size), 0) + lax.axis_index("col") * half
    return lax.broadcasted_iota(jnp.int32, (half, size), 1) == rows


def pack_halo(dims, tail_parity, x_ref, out_ref):
    rows, width = dims[:2]
    for parity in (0, 1):

        @pl.when(lax.axis_index("row") % 2 == parity)
        def _(parity=parity):
            blocks = tail_blocks(rows, width) if parity == tail_parity else head_blocks(width)
            for n, (row, d) in enumerate(blocks):
                out_ref[n] = x_ref[row, d]


def start_kernel(
    dims, reach_hbm, bounds_hbm, flag_hbm, h_hbm, x_ref, near_ref, part_ref, h_ref, reach_ref, bounds_ref,
    flag_ref, in_sems, small_sems,
):
    rows, width, half, size = dims
    first_row = lax.axis_index("row") * rows
    total_rows = lax.axis_size("row") * rows
    small = [
        pltpu.make_async_copy(src, dst, small_sems.at[n])
        for n, (src, dst) in enumerate(((reach_hbm, reach_ref), (bounds_hbm, bounds_ref), (flag_hbm, flag_ref)))
    ]
    large = [pltpu.make_async_copy(h_hbm.at[i], h_ref.at[i], in_sems.at[i]) for i in range(rows)]
    for copy in small + large:
        copy.start()
    on_diag = diag_mask(half, size)

    def fold(block):
        return jnp.sum(block.reshape(half // LINES, LINES, size), axis=0)

    for copy in small:
        copy.wait()
    diag = jnp.zeros((LINES, size), F32)
    once = jnp.zeros((LINES, size), F32)
    twice = jnp.zeros((LINES, size), F32)
    for row in range(rows):
        large[row].wait()
        for d in range(width + 1):
            kept = is_kept(reach_ref, row, d, first_row, total_rows)
            x = start_block(h_ref[row, d], d, kept, bounds_ref, on_diag)
            x_ref[row, d] = x
            wide = x.astype(F32)
            if d == 0:
                diag = diag + fold(jnp.where(on_diag, wide, 0.0))
                once = once + fold(wide * wide)
            else:
                twice = twice + fold(wide * wide)
    norm = once + 2.0 * twice
    part = jnp.where(flag_ref[0] == 1, norm, 2.0 * diag - norm)
    part_ref[...] = part

    pack_halo(dims, 0, x_ref, near_ref)

def strips(rows, width):
    out = []
    for j in range(0, rows + width, 2):
        cols = list(range(j, min(j + 2, rows + width)))
        i_lo, i_hi = max(0, j - width), min(rows - 1, cols[-1])
        k_lo = max(0, j - width)
        k_hi = min(rows + width - 1 if j < rows else rows - 1, cols[-1] + width, i_hi + width)
        out.append((cols, i_lo, i_hi, k_lo, k_hi))
    return out


def inner_kernel(dims, first, last, reach_ref, flag_ref, mine_ref, other_ref, out_hbm, out_ref, full, left, sems):
    rows, width, half, size = dims
    column = lax.axis_index("col")
    first_row = lax.axis_index("row") * rows
    total_rows = lax.axis_size("row") * rows
    mine = pl.multiple_of(column * half, half)
    other = pl.multiple_of((1 - column) * half, half)
    jobs = strips(rows, width)[first:last]

    def block(n):
        return pl.ds(n * size, size)

    need_full, need_left = set(), set()
    for cols, i_lo, i_hi, k_lo, k_hi in jobs:
        need_full |= {(k, j) for k in range(k_lo, k_hi + 1) for j in cols}
        need_left |= {(i, k) for i in range(i_lo, i_hi + 1) for k in range(k_lo, k_hi + 1)}
    below = {(k, j) for k, j in need_full if j < k <= j + width}
    turned = below | {(i, k) for i, k in need_left if k < i <= k + width}
    for k, j in sorted({(k, j) for k, j in need_full if k <= j <= k + width} | {(j, k) for k, j in turned}):
        full[pl.ds(k * size + mine, half), block(j)] = mine_ref[k, j - k]
        full[pl.ds(k * size + other, half), block(j)] = other_ref[k, j - k]
    for k, j in sorted(turned):
        full[block(k), block(j)] = full[block(j), block(k)].T
    for k, j in sorted(need_full):
        if abs(k - j) > width:
            full[block(k), block(j)] = jnp.zeros((size, size), BF16)
    for i, k in sorted(need_left):
        if abs(i - k) > width:
            piece = jnp.zeros((half, size), BF16)
        elif k >= i:
            piece = mine_ref[i, k - i]
        else:
            piece = full[pl.ds(i * size + mine, half), block(k)]
        left[pl.ds(i * half, half), block(k)] = piece

    sign = jnp.where(flag_ref[0] == 1, 1.0, -1.0)
    twice = jnp.where(flag_ref[0] == 1, 0.0, 2.0)
    copies = []
    for cols, i_lo, i_hi, k_lo, k_hi in jobs:
        depth = pl.ds(k_lo * size, (k_hi - k_lo + 1) * size)
        square = jnp.dot(
            left[pl.ds(i_lo * half, (i_hi - i_lo + 1) * half), depth],
            full[depth, pl.ds(cols[0] * size, len(cols) * size)],
            preferred_element_type=F32,
        )
        for i in range(i_lo, i_hi + 1):
            ready = [j - i for j in cols if 0 <= j - i <= width]
            for d in ready:
                n = i + d - cols[0]
                kept = is_kept(reach_ref, i, d, first_row, total_rows)
                part = square[(i - i_lo) * half : (i - i_lo + 1) * half, n * size : (n + 1) * size]
                out_ref[i, d] = part * jnp.where(kept, sign, 0.0) + twice * mine_ref[i, d].astype(F32)
            if ready:
                run = pl.ds(ready[0], len(ready))
                copies.append(pltpu.make_async_copy(out_ref.at[i, run], out_hbm.at[i, run], sems.at[len(copies)]))
                copies[-1].start()
    for copy in copies:
        copy.wait()


def inner_first_kernel(dims, cut, reach_ref, flag_ref, mine_ref, other_ref, out_hbm, far_ref, *scratch):
    pack_halo(dims, 1, mine_ref, far_ref)
    inner_kernel(dims, 0, cut, reach_ref, flag_ref, mine_ref, other_ref, out_hbm, *scratch)


def inner_last_kernel(dims, cut, reach_ref, flag_ref, mine_ref, other_ref, base_hbm, out_hbm, *scratch):
    inner_kernel(dims, cut, None, reach_ref, flag_ref, mine_ref, other_ref, out_hbm, *scratch)


def fetch(base_ref, held, jobs, sems):
    copies = []
    for n, (row, d, count, at) in enumerate(jobs):
        copies.append(pltpu.make_async_copy(base_ref.at[row, pl.ds(d, count)], held.at[pl.ds(at, count)], sems.at[n]))
        copies[-1].start()
    return copies


def finish(dims, reach_ref, flag_ref, square, from_row, from_col, copies, jobs, held, out_ref, sems):
    rows, width, half, size = dims
    first_row = lax.axis_index("row") * rows
    total_rows = lax.axis_size("row") * rows
    sign = jnp.where(flag_ref[0] == 1, 1.0, -1.0)
    backs = []
    for n, (row, d, count, at) in enumerate(jobs):
        copies[n].wait()
        for e in range(count):
            i, j = row - from_row, row + d + e - from_col
            kept = is_kept(reach_ref, row, d + e, first_row, total_rows)
            part = square[i * half : (i + 1) * half, j * size : (j + 1) * size]
            held[at + e] = held[at + e] + part * jnp.where(kept, sign, 0.0)
        copy = pltpu.make_async_copy(held.at[pl.ds(at, count)], out_ref.at[row, pl.ds(d, count)], sems.at[n])
        copy.start()
        backs.append(copy)
    for copy in backs:
        copy.wait()


def halves(dims):
    half = dims[2]
    column = lax.axis_index("col")
    return pl.multiple_of(column * half, half), pl.multiple_of((1 - column) * half, half)


def add_above(dims, reach_ref, flag_ref, mine_ref, other_ref, base_ref, out_ref, whole, turned, left, held, in_sems, out_sems):
    rows, width, half, size = dims
    mine, other = halves(dims)
    jobs = runs(head_blocks(width))
    copies = fetch(base_ref, held, jobs, in_sems)

    def block(n):
        return pl.ds(n * size, size)

    have = set()
    for n, (row, d) in enumerate(tail_blocks(rows, width)):
        k, j = row - rows + width, row + d - rows
        whole[pl.ds(k * size + mine, half), block(j)] = mine_ref[n]
        whole[pl.ds(k * size + other, half), block(j)] = other_ref[n]
        have.add((k, j))
    for k in range(width):
        for j in range(width):
            if (k, j) in have:
                turned[block(j), block(k)] = whole[block(k), block(j)].T
                left[pl.ds(j * half, half), block(k)] = turned[pl.ds(j * size + mine, half), block(k)]
            else:
                whole[block(k), block(j)] = jnp.zeros((size, size), BF16)
                left[pl.ds(j * half, half), block(k)] = jnp.zeros((half, size), BF16)
    square = jnp.dot(left[...], whole[...], preferred_element_type=F32)
    finish(dims, reach_ref, flag_ref, square, 0, 0, copies, jobs, held, out_ref, out_sems)


def add_below(dims, reach_ref, flag_ref, mine_ref, other_ref, sent_ref, base_ref, out_ref, whole, left, held, in_sems, out_sems):
    rows, width, half, size = dims
    mine, other = halves(dims)
    jobs = runs(tail_blocks(rows, width))
    copies = fetch(base_ref, held, jobs, in_sems)

    def block(n):
        return pl.ds(n * size, size)

    have = set()
    for n, (row, d) in enumerate(tail_blocks(rows, width)):
        i, k = row - rows + width, row + d - rows
        left[pl.ds(i * half, half), block(k)] = sent_ref[n]
        have.add((i, k))
    for i in range(width):
        for k in range(width):
            if (i, k) not in have:
                left[pl.ds(i * half, half), block(k)] = jnp.zeros((half, size), BF16)
    for n, (k, d) in enumerate(head_blocks(width)):
        whole[pl.ds(k * size + mine, half), block(k + d)] = mine_ref[n]
        whole[pl.ds(k * size + other, half), block(k + d)] = other_ref[n]
        if d:
            whole[block(k + d), block(k)] = whole[block(k), block(k + d)].T
    square = jnp.dot(left[...], whole[...], preferred_element_type=F32)
    finish(dims, reach_ref, flag_ref, square, rows - width, rows, copies, jobs, held, out_ref, out_sems)


def halo_kernel(
    dims, above_parity, reach_ref, flag_ref, mine_ref, other_ref, sent_ref, trace_ref, got_ref, base_ref, out_ref, sum_ref,
    whole, turned, left, held, sems,
):
    total = jnp.sum(trace_ref[...] + got_ref[...])
    sum_ref[0] = total / (lax.axis_size("row") * dims[0] * dims[3])
    parity = lax.axis_index("row") % 2

    @pl.when(parity == above_parity)
    def _():
        add_above(
            dims, reach_ref, flag_ref, mine_ref, other_ref, base_ref, out_ref, whole, turned, left, held, sems.at[0], sems.at[1]
        )

    @pl.when(parity != above_parity)
    def _():
        add_below(
            dims, reach_ref, flag_ref, mine_ref, other_ref, sent_ref, base_ref, out_ref, whole, left, held, sems.at[0], sems.at[1]
        )


def per_device(hamiltonian, bounds, block_reach, branch_flags):
    rows, offsets, half, size = hamiltonian.shape
    width = offsets - 1
    dims = (rows, width, half, size)
    halo = len(head_blocks(width))
    count = lax.axis_size("row")
    near_pairs = [(i, i ^ 1) for i in range(count)]
    far_pairs = [(i, j) for i in range(count) for j in [((i + 1) ^ 1) - 1] if 0 <= j < count]
    swap = [(0, 1), (1, 0)]
    whole = jax.ShapeDtypeStruct(hamiltonian.shape, F32)
    packed = jax.ShapeDtypeStruct((halo, half, size), BF16)

    current, near, part = pl.pallas_call(
        functools.partial(start_kernel, dims),
        out_shape=(
            jax.ShapeDtypeStruct(hamiltonian.shape, BF16),
            packed,
            jax.ShapeDtypeStruct((LINES, size), F32),
        ),
        in_specs=[HBM, HBM, HBM, HBM],
        out_specs=(VMEM, VMEM, VMEM),
        scratch_shapes=[
            pltpu.VMEM(hamiltonian.shape, F32),
            pltpu.SMEM(block_reach.shape, jnp.int32),
            pltpu.SMEM(bounds.shape, F32),
            pltpu.SMEM(branch_flags.shape, jnp.int32),
            pltpu.SemaphoreType.DMA((rows,)),
            pltpu.SemaphoreType.DMA((3,)),
        ],
        compiler_params=pltpu.CompilerParams(vmem_limit_bytes=51 * MIB),
        cost_estimate=SMALL,
        name="start",
    )(block_reach, bounds, branch_flags, hamiltonian)
    swapped = lax.ppermute(current, "col", swap)
    near_mine = lax.ppermute(near, "row", near_pairs)
    steps = [1 << n for n in reversed(range(count.bit_length() - 1))]
    trace, got = part, jnp.zeros_like(part)
    for step in steps[:-2]:
        trace = trace + got
        got = lax.ppermute(trace, "row", [(i, i ^ step) for i in range(count)])

    cut = CUT
    inner_scratch = [
        pltpu.VMEM(hamiltonian.shape, F32),
        pltpu.VMEM(((rows + width) * size, (rows + width) * size), BF16),
        pltpu.VMEM((rows * half, (rows + width) * size), BF16),
        pltpu.SemaphoreType.DMA((rows * (rows + width),)),
    ]
    base, far = pl.pallas_call(
        functools.partial(inner_first_kernel, dims, cut),
        out_shape=(whole, packed),
        in_specs=[SMEM, SMEM, VMEM, VMEM],
        out_specs=(HBM, VMEM),
        scratch_shapes=inner_scratch,
        compiler_params=pltpu.CompilerParams(vmem_limit_bytes=24 * MIB),
        cost_estimate=SMALL,
        name="inner_first",
    )(block_reach, branch_flags, current, swapped)
    far_mine = lax.ppermute(far, "row", far_pairs)
    base, near_mine, got = lax.optimization_barrier((base, near_mine, got))
    near_other = lax.ppermute(near_mine, "col", swap)
    trace = trace + got
    got = lax.ppermute(trace, "row", [(i, i ^ 2) for i in range(count)])
    base = pl.pallas_call(
        functools.partial(inner_last_kernel, dims, cut),
        out_shape=whole,
        in_specs=[SMEM, SMEM, VMEM, VMEM, HBM],
        out_specs=HBM,
        input_output_aliases={4: 0},
        scratch_shapes=inner_scratch,
        compiler_params=pltpu.CompilerParams(vmem_limit_bytes=24 * MIB),
        cost_estimate=SMALL,
        name="inner_last",
    )(block_reach, branch_flags, current, swapped, base)
    base, got = lax.optimization_barrier((base, got))
    trace = trace + got
    got = lax.ppermute(trace, "row", [(i, i ^ 1) for i in range(count)])

    def add_halo(above_parity, mine, other, sent, trace, got, base):
        square = pltpu.VMEM((width * size, width * size), BF16)
        return pl.pallas_call(
            functools.partial(halo_kernel, dims, above_parity),
            out_shape=(whole, jax.ShapeDtypeStruct((1,), F32)),
            in_specs=[SMEM, SMEM, VMEM, VMEM, VMEM, VMEM, VMEM, ANY],
            out_specs=(ANY, SMEM),
            input_output_aliases={7: 0},
            scratch_shapes=[
                square, square, pltpu.VMEM((width * half, width * size), BF16), pltpu.VMEM((halo, half, size), F32),
                pltpu.SemaphoreType.DMA((2, width)),
            ],
            compiler_params=pltpu.CompilerParams(vmem_limit_bytes=16 * MIB),
            cost_estimate=SMALL,
            name="halo",
        )(block_reach, branch_flags, mine, other, sent, trace, got, base)

    base, _ = add_halo(1, near_mine, near_other, near, part, part, base)
    base, far_mine, got = lax.optimization_barrier((base, far_mine, got))
    far_other = lax.ppermute(far_mine, "col", swap)
    trace = trace + got
    got = lax.ppermute(trace, "col", swap)
    return add_halo(0, far_mine, far_other, far, trace, got, base)


def solution(mesh):
    placed = (
        P(("groups", "row"), None, "col", None),
        P("groups"),
        P(("groups", "row")),
        P("groups"),
    )
    return jax.shard_map(
        per_device,
        mesh=mesh,
        in_specs=placed,
        out_specs=(P(("groups", "row"), None, "col", None), P("groups")),
        check_vma=False,
    )
```

```python
import functools

import jax
import jax.numpy as jnp
from jax import lax
from jax.experimental import pallas as pl
from jax.experimental.pallas import tpu as pltpu
from jax.sharding import PartitionSpec as P

SMEM = pl.BlockSpec(memory_space=pltpu.SMEM)
VMEM = pl.BlockSpec(memory_space=pltpu.VMEM)
ANY = pl.BlockSpec(memory_space=pl.ANY)
HBM = pl.BlockSpec(memory_space=pltpu.HBM)
F32 = jnp.float32
BF16 = jnp.bfloat16
MIB = 1 << 20
LINES = 64
PAD = 1
SMALL = pl.CostEstimate(flops=1, bytes_accessed=1, transcendentals=0)


def tail_blocks(rows, width):
    return [(rows - m, d) for m in range(1, width + 1) for d in range(m, width + 1)]


def head_blocks(width):
    return [(m, d) for m in range(width) for d in range(width - m)]


def runs(blocks):
    out = []
    for place, (row, d) in enumerate(blocks):
        if out and out[-1][0] == row:
            out[-1][2] += 1
        else:
            out.append([row, d, 1, place])
    return out


def is_kept(reach_ref, row, d, first_row, total_rows):
    return (d <= reach_ref[row]) & (first_row + row + d < total_rows)


def start_block(h, d, kept, bounds_ref, on_diag):
    high = bounds_ref[1]
    scale = jnp.where(kept, 1.0, 0.0) / (high + bounds_ref[0])
    if d == 0:
        return ((jnp.where(on_diag, high, 0.0) - h) * scale).astype(BF16)
    return (h * -scale).astype(BF16)


def diag_mask(half, size):
    rows = lax.broadcasted_iota(jnp.int32, (half, size), 0) + lax.axis_index("col") * half
    return lax.broadcasted_iota(jnp.int32, (half, size), 1) == rows


def pack_halo(dims, tail_parity, x_ref, out_ref):
    rows, width = dims[:2]
    for parity in (0, 1):

        @pl.when(lax.axis_index("row") % 2 == parity)
        def _(parity=parity):
            blocks = tail_blocks(rows, width) if parity == tail_parity else head_blocks(width)
            for n, (row, d) in enumerate(blocks):
                out_ref[n] = x_ref[row, d]
    for n in range(len(head_blocks(width)), out_ref.shape[0]):
        out_ref[n] = jnp.zeros(out_ref.shape[1:], BF16)


def start_kernel(
    dims, reach_hbm, bounds_hbm, flag_hbm, h_hbm, x_ref, near_ref, far_ref, part_ref, h_ref, reach_ref, bounds_ref,
    flag_ref, in_sems, small_sems,
):
    rows, width, half, size = dims
    first_row = lax.axis_index("row") * rows
    total_rows = lax.axis_size("row") * rows
    small = [
        pltpu.make_async_copy(src, dst, small_sems.at[n])
        for n, (src, dst) in enumerate(((reach_hbm, reach_ref), (bounds_hbm, bounds_ref), (flag_hbm, flag_ref)))
    ]
    large = [pltpu.make_async_copy(h_hbm.at[i], h_ref.at[i], in_sems.at[i]) for i in range(rows)]
    for copy in small + large:
        copy.start()
    on_diag = diag_mask(half, size)

    def fold(block):
        return jnp.sum(block.reshape(half // LINES, LINES, size), axis=0)

    for copy in small:
        copy.wait()
    diag = jnp.zeros((LINES, size), F32)
    once = jnp.zeros((LINES, size), F32)
    twice = jnp.zeros((LINES, size), F32)
    for row in range(rows):
        large[row].wait()
        for d in range(width + 1):
            kept = is_kept(reach_ref, row, d, first_row, total_rows)
            x = start_block(h_ref[row, d], d, kept, bounds_ref, on_diag)
            x_ref[row, d] = x
            wide = x.astype(F32)
            if d == 0:
                diag = diag + fold(jnp.where(on_diag, wide, 0.0))
                once = once + fold(wide * wide)
            else:
                twice = twice + fold(wide * wide)
    norm = once + 2.0 * twice
    part = jnp.where(flag_ref[0] == 1, norm, 2.0 * diag - norm)
    part_ref[...] = part

    pack_halo(dims, 0, x_ref, near_ref)
    pack_halo(dims, 1, x_ref, far_ref)

def strips(rows, width):
    out = []
    for j in range(0, rows + width, 2):
        cols = list(range(j, min(j + 2, rows + width)))
        i_lo, i_hi = max(0, j - width), min(rows - 1, cols[-1])
        k_lo = max(0, j - width)
        k_hi = min(rows + width - 1 if j < rows else rows - 1, cols[-1] + width, i_hi + width)
        out.append((cols, i_lo, i_hi, k_lo, k_hi))
    return out


def inner_kernel(dims, reach_ref, flag_ref, mine_ref, other_ref, out_hbm, out_ref, full, left, sems):
    rows, width, half, size = dims
    column = lax.axis_index("col")
    first_row = lax.axis_index("row") * rows
    total_rows = lax.axis_size("row") * rows
    mine = pl.multiple_of(column * half, half)
    other = pl.multiple_of((1 - column) * half, half)
    jobs = strips(rows, width)

    def block(n):
        return pl.ds(n * size, size)

    need_full, need_left = set(), set()
    for cols, i_lo, i_hi, k_lo, k_hi in jobs:
        need_full |= {(k, j) for k in range(k_lo, k_hi + 1) for j in cols}
        need_left |= {(i, k) for i in range(i_lo, i_hi + 1) for k in range(k_lo, k_hi + 1)}
    below = {(k, j) for k, j in need_full if j < k <= j + width}
    turned = below | {(i, k) for i, k in need_left if k < i <= k + width}
    for k, j in sorted({(k, j) for k, j in need_full if k <= j <= k + width} | {(j, k) for k, j in turned}):
        full[pl.ds(k * size + mine, half), block(j)] = mine_ref[k, j - k]
        full[pl.ds(k * size + other, half), block(j)] = other_ref[k, j - k]
    for k, j in sorted(turned):
        full[block(k), block(j)] = full[block(j), block(k)].T
    for k, j in sorted(need_full):
        if abs(k - j) > width:
            full[block(k), block(j)] = jnp.zeros((size, size), BF16)
    for i, k in sorted(need_left):
        if abs(i - k) > width:
            piece = jnp.zeros((half, size), BF16)
        elif k >= i:
            piece = mine_ref[i, k - i]
        else:
            piece = full[pl.ds(i * size + mine, half), block(k)]
        left[pl.ds(i * half, half), block(k)] = piece

    sign = jnp.where(flag_ref[0] == 1, 1.0, -1.0)
    twice = jnp.where(flag_ref[0] == 1, 0.0, 2.0)
    copies = []
    for cols, i_lo, i_hi, k_lo, k_hi in jobs:
        depth = pl.ds(k_lo * size, (k_hi - k_lo + 1) * size)
        square = jnp.dot(
            left[pl.ds(i_lo * half, (i_hi - i_lo + 1) * half), depth],
            full[depth, pl.ds(cols[0] * size, len(cols) * size)],
            preferred_element_type=F32,
        )
        for i in range(i_lo, i_hi + 1):
            for d in [j - i for j in cols if 0 <= j - i <= width]:
                n = i + d - cols[0]
                kept = is_kept(reach_ref, i, d, first_row, total_rows)
                part = square[(i - i_lo) * half : (i - i_lo + 1) * half, n * size : (n + 1) * size]
                out_ref[i, d] = part * jnp.where(kept, sign, 0.0) + twice * mine_ref[i, d].astype(F32)
                if d == width:
                    copies.append(pltpu.make_async_copy(out_ref.at[i], out_hbm.at[i], sems.at[i]))
                    copies[-1].start()
    for copy in copies:
        copy.wait()


def fetch(base_ref, held, jobs, sems):
    copies = []
    for n, (row, d, count, at) in enumerate(jobs):
        copies.append(pltpu.make_async_copy(base_ref.at[row, pl.ds(d, count)], held.at[pl.ds(at, count)], sems.at[n]))
        copies[-1].start()
    return copies


def finish(dims, reach_ref, flag_ref, square, from_row, from_col, copies, jobs, held, out_ref, sems):
    rows, width, half, size = dims
    first_row = lax.axis_index("row") * rows
    total_rows = lax.axis_size("row") * rows
    sign = jnp.where(flag_ref[0] == 1, 1.0, -1.0)
    backs = []
    for n, (row, d, count, at) in enumerate(jobs):
        copies[n].wait()
        for e in range(count):
            i, j = row - from_row, row + d + e - from_col
            kept = is_kept(reach_ref, row, d + e, first_row, total_rows)
            part = square[i * half : (i + 1) * half, j * size : (j + 1) * size]
            held[at + e] = held[at + e] + part * jnp.where(kept, sign, 0.0)
        copy = pltpu.make_async_copy(held.at[pl.ds(at, count)], out_ref.at[row, pl.ds(d, count)], sems.at[n])
        copy.start()
        backs.append(copy)
    for copy in backs:
        copy.wait()


def halves(dims):
    half = dims[2]
    column = lax.axis_index("col")
    return pl.multiple_of(column * half, half), pl.multiple_of((1 - column) * half, half)


def add_above(dims, reach_ref, flag_ref, mine_ref, other_ref, base_ref, out_ref, whole, turned, left, held, in_sems, out_sems):
    rows, width, half, size = dims
    mine, other = halves(dims)
    jobs = runs(head_blocks(width))
    copies = fetch(base_ref, held, jobs, in_sems)

    def block(n):
        return pl.ds(n * size, size)

    have = set()
    for n, (row, d) in enumerate(tail_blocks(rows, width)):
        k, j = row - rows + width, row + d - rows
        whole[pl.ds(k * size + mine, half), block(j)] = mine_ref[n]
        whole[pl.ds(k * size + other, half), block(j)] = other_ref[n]
        have.add((k, j))
    for k in range(width):
        for j in range(width):
            if (k, j) in have:
                turned[block(j), block(k)] = whole[block(k), block(j)].T
                left[pl.ds(j * half, half), block(k)] = turned[pl.ds(j * size + mine, half), block(k)]
            else:
                whole[block(k), block(j)] = jnp.zeros((size, size), BF16)
                left[pl.ds(j * half, half), block(k)] = jnp.zeros((half, size), BF16)
    square = jnp.dot(left[...], whole[...], preferred_element_type=F32)
    finish(dims, reach_ref, flag_ref, square, 0, 0, copies, jobs, held, out_ref, out_sems)


def add_below(dims, reach_ref, flag_ref, mine_ref, other_ref, sent_ref, base_ref, out_ref, whole, left, held, in_sems, out_sems):
    rows, width, half, size = dims
    mine, other = halves(dims)
    jobs = runs(tail_blocks(rows, width))
    copies = fetch(base_ref, held, jobs, in_sems)

    def block(n):
        return pl.ds(n * size, size)

    have = set()
    for n, (row, d) in enumerate(tail_blocks(rows, width)):
        i, k = row - rows + width, row + d - rows
        left[pl.ds(i * half, half), block(k)] = sent_ref[n]
        have.add((i, k))
    for i in range(width):
        for k in range(width):
            if (i, k) not in have:
                left[pl.ds(i * half, half), block(k)] = jnp.zeros((half, size), BF16)
    for n, (k, d) in enumerate(head_blocks(width)):
        whole[pl.ds(k * size + mine, half), block(k + d)] = mine_ref[n]
        whole[pl.ds(k * size + other, half), block(k + d)] = other_ref[n]
        if d:
            whole[block(k + d), block(k)] = whole[block(k), block(k + d)].T
    square = jnp.dot(left[...], whole[...], preferred_element_type=F32)
    finish(dims, reach_ref, flag_ref, square, rows - width, rows, copies, jobs, held, out_ref, out_sems)


def halo_kernel(
    dims, above_parity, reach_ref, flag_ref, mine_ref, other_ref, sent_ref, trace_ref, base_ref, out_ref, sum_ref,
    whole, turned, left, held, sems,
):
    total = jnp.sum(trace_ref[...])
    sum_ref[0] = total / (lax.axis_size("row") * dims[0] * dims[3])
    parity = lax.axis_index("row") % 2

    @pl.when(parity == above_parity)
    def _():
        add_above(
            dims, reach_ref, flag_ref, mine_ref, other_ref, base_ref, out_ref, whole, turned, left, held, sems.at[0], sems.at[1]
        )

    @pl.when(parity != above_parity)
    def _():
        add_below(
            dims, reach_ref, flag_ref, mine_ref, other_ref, sent_ref, base_ref, out_ref, whole, left, held, sems.at[0], sems.at[1]
        )


def per_device(hamiltonian, bounds, block_reach, branch_flags):
    rows, offsets, half, size = hamiltonian.shape
    width = offsets - 1
    dims = (rows, width, half, size)
    halo = len(head_blocks(width))
    count = lax.axis_size("row")
    near_pairs = [(i, i ^ 1) for i in range(count)]
    far_pairs = [(i, j) for i in range(count) for j in [((i + 1) ^ 1) - 1] if 0 <= j < count]
    swap = [(0, 1), (1, 0)]
    whole = jax.ShapeDtypeStruct(hamiltonian.shape, F32)
    packed = jax.ShapeDtypeStruct((halo, half, size), BF16)

    current, near, far, part = pl.pallas_call(
        functools.partial(start_kernel, dims),
        out_shape=(
            jax.ShapeDtypeStruct(hamiltonian.shape, BF16),
            packed,
            jax.ShapeDtypeStruct((halo + PAD, half, size), BF16),
            jax.ShapeDtypeStruct((LINES, size), F32),
        ),
        in_specs=[HBM, HBM, HBM, HBM],
        out_specs=(VMEM, VMEM, VMEM, VMEM),
        scratch_shapes=[
            pltpu.VMEM(hamiltonian.shape, F32),
            pltpu.SMEM(block_reach.shape, jnp.int32),
            pltpu.SMEM(bounds.shape, F32),
            pltpu.SMEM(branch_flags.shape, jnp.int32),
            pltpu.SemaphoreType.DMA((rows,)),
            pltpu.SemaphoreType.DMA((3,)),
        ],
        compiler_params=pltpu.CompilerParams(vmem_limit_bytes=50 * MIB),
        cost_estimate=SMALL,
        name="start",
    )(block_reach, bounds, branch_flags, hamiltonian)
    swapped = lax.ppermute(current, "col", swap)
    near_mine = lax.ppermute(near, "row", near_pairs)
    parts = lax.all_gather(part, ("row", "col"), tiled=True)
    far_mine = lax.ppermute(far, "row", far_pairs)
    base = pl.pallas_call(
        functools.partial(inner_kernel, dims),
        out_shape=whole,
        in_specs=[SMEM, SMEM, VMEM, VMEM],
        out_specs=HBM,
        scratch_shapes=[
            pltpu.VMEM(hamiltonian.shape, F32),
            pltpu.VMEM(((rows + width) * size, (rows + width) * size), BF16),
            pltpu.VMEM((rows * half, (rows + width) * size), BF16),
            pltpu.SemaphoreType.DMA((rows,)),
        ],
        compiler_params=pltpu.CompilerParams(vmem_limit_bytes=24 * MIB),
        cost_estimate=SMALL,
        name="inner",
    )(block_reach, branch_flags, current, swapped)
    base, near_mine = lax.optimization_barrier((base, near_mine))
    near_other = lax.ppermute(near_mine, "col", swap)

    def add_halo(above_parity, mine, other, sent, trace, base):
        square = pltpu.VMEM((width * size, width * size), BF16)
        return pl.pallas_call(
            functools.partial(halo_kernel, dims, above_parity),
            out_shape=(whole, jax.ShapeDtypeStruct((1,), F32)),
            in_specs=[SMEM, SMEM, VMEM, VMEM, VMEM, VMEM, ANY],
            out_specs=(ANY, SMEM),
            input_output_aliases={6: 0},
            scratch_shapes=[
                square, square, pltpu.VMEM((width * half, width * size), BF16), pltpu.VMEM((halo, half, size), F32),
                pltpu.SemaphoreType.DMA((2, width)),
            ],
            compiler_params=pltpu.CompilerParams(vmem_limit_bytes=16 * MIB),
            cost_estimate=SMALL,
            name="halo",
        )(block_reach, branch_flags, mine, other, sent, trace, base)

    base, _ = add_halo(1, near_mine, near_other, near, part, base)
    base, far_mine, parts = lax.optimization_barrier((base, far_mine, parts))
    far_other = lax.ppermute(far_mine, "col", swap)
    return add_halo(0, far_mine, far_other, far, parts, base)


def solution(mesh):
    placed = (
        P(("groups", "row"), None, "col", None),
        P("groups"),
        P(("groups", "row")),
        P("groups"),
    )
    return jax.shard_map(
        per_device,
        mesh=mesh,
        in_specs=placed,
        out_specs=(P(("groups", "row"), None, "col", None), P("groups")),
        check_vma=False,
    )
```

```python
import functools

import jax
import jax.numpy as jnp
from jax import lax
from jax.experimental import pallas as pl
from jax.experimental.pallas import tpu as pltpu
from jax.sharding import PartitionSpec as P

SMEM = pl.BlockSpec(memory_space=pltpu.SMEM)
VMEM = pl.BlockSpec(memory_space=pltpu.VMEM)
ANY = pl.BlockSpec(memory_space=pl.ANY)
HBM = pl.BlockSpec(memory_space=pltpu.HBM)
F32 = jnp.float32
BF16 = jnp.bfloat16
MIB = 1 << 20
LINES = 16
SMALL = pl.CostEstimate(flops=1, bytes_accessed=1, transcendentals=0)


def tail_blocks(rows, width):
    return [(rows - m, d) for m in range(1, width + 1) for d in range(m, width + 1)]


def head_blocks(width):
    return [(m, d) for m in range(width) for d in range(width - m)]


def runs(blocks):
    out = []
    for place, (row, d) in enumerate(blocks):
        if out and out[-1][0] == row:
            out[-1][2] += 1
        else:
            out.append([row, d, 1, place])
    return out


def is_kept(reach_ref, row, d, first_row, total_rows):
    return (d <= reach_ref[row]) & (first_row + row + d < total_rows)


def start_block(h, d, kept, bounds_ref, on_diag):
    high = bounds_ref[1]
    scale = jnp.where(kept, 1.0, 0.0) / (high + bounds_ref[0])
    if d == 0:
        return ((jnp.where(on_diag, high, 0.0) - h) * scale).astype(BF16)
    return (h * -scale).astype(BF16)


def diag_mask(half, size):
    rows = lax.broadcasted_iota(jnp.int32, (half, size), 0) + lax.axis_index("col") * half
    return lax.broadcasted_iota(jnp.int32, (half, size), 1) == rows


def pack_halo(dims, tail_parity, x_ref, out_ref):
    rows, width = dims[:2]
    for parity in (0, 1):

        @pl.when(lax.axis_index("row") % 2 == parity)
        def _(parity=parity):
            blocks = tail_blocks(rows, width) if parity == tail_parity else head_blocks(width)
            for n, (row, d) in enumerate(blocks):
                out_ref[n] = x_ref[row, d]


def pack_far_kernel(dims, x_ref, sum_ref, out_ref):
    rows, width, half, size = dims
    pack_halo(dims, 1, x_ref, out_ref)
    rest = sum_ref[...]
    for n in range(half // LINES):
        term = rest.astype(BF16) if n < 3 else jnp.zeros((LINES, size), BF16)
        out_ref[out_ref.shape[0] - 1, pl.ds(n * LINES, LINES)] = term
        rest = rest - term.astype(F32)


def start_kernel(
    dims, reach_hbm, bounds_hbm, flag_hbm, h_hbm, x_ref, near_ref, part_ref, h_ref, reach_ref, bounds_ref,
    flag_ref, in_sems, small_sems,
):
    rows, width, half, size = dims
    first_row = lax.axis_index("row") * rows
    total_rows = lax.axis_size("row") * rows
    small = [
        pltpu.make_async_copy(src, dst, small_sems.at[n])
        for n, (src, dst) in enumerate(((reach_hbm, reach_ref), (bounds_hbm, bounds_ref), (flag_hbm, flag_ref)))
    ]
    large = [pltpu.make_async_copy(h_hbm.at[i], h_ref.at[i], in_sems.at[i]) for i in range(rows)]
    for copy in small + large:
        copy.start()
    on_diag = diag_mask(half, size)

    def fold(block):
        return jnp.sum(block.reshape(half // LINES, LINES, size), axis=0)

    for copy in small:
        copy.wait()
    diag = jnp.zeros((LINES, size), F32)
    once = jnp.zeros((LINES, size), F32)
    twice = jnp.zeros((LINES, size), F32)
    for row in range(rows):
        large[row].wait()
        for d in range(width + 1):
            kept = is_kept(reach_ref, row, d, first_row, total_rows)
            x = start_block(h_ref[row, d], d, kept, bounds_ref, on_diag)
            x_ref[row, d] = x
            wide = x.astype(F32)
            if d == 0:
                diag = diag + fold(jnp.where(on_diag, wide, 0.0))
                once = once + fold(wide * wide)
            else:
                twice = twice + fold(wide * wide)
    norm = once + 2.0 * twice
    part = jnp.where(flag_ref[0] == 1, norm, 2.0 * diag - norm)
    part_ref[...] = part

    pack_halo(dims, 0, x_ref, near_ref)

def strips(rows, width):
    out = []
    for j in range(0, rows + width, 2):
        cols = list(range(j, min(j + 2, rows + width)))
        i_lo, i_hi = max(0, j - width), min(rows - 1, cols[-1])
        k_lo = max(0, j - width)
        k_hi = min(rows + width - 1 if j < rows else rows - 1, cols[-1] + width, i_hi + width)
        out.append((cols, i_lo, i_hi, k_lo, k_hi))
    return out


def inner_kernel(dims, reach_ref, flag_ref, mine_ref, other_ref, out_hbm, out_ref, full, left, sems):
    rows, width, half, size = dims
    column = lax.axis_index("col")
    first_row = lax.axis_index("row") * rows
    total_rows = lax.axis_size("row") * rows
    mine = pl.multiple_of(column * half, half)
    other = pl.multiple_of((1 - column) * half, half)
    jobs = strips(rows, width)

    def block(n):
        return pl.ds(n * size, size)

    need_full, need_left = set(), set()
    for cols, i_lo, i_hi, k_lo, k_hi in jobs:
        need_full |= {(k, j) for k in range(k_lo, k_hi + 1) for j in cols}
        need_left |= {(i, k) for i in range(i_lo, i_hi + 1) for k in range(k_lo, k_hi + 1)}
    below = {(k, j) for k, j in need_full if j < k <= j + width}
    turned = below | {(i, k) for i, k in need_left if k < i <= k + width}
    for k, j in sorted({(k, j) for k, j in need_full if k <= j <= k + width} | {(j, k) for k, j in turned}):
        full[pl.ds(k * size + mine, half), block(j)] = mine_ref[k, j - k]
        full[pl.ds(k * size + other, half), block(j)] = other_ref[k, j - k]
    for k, j in sorted(turned):
        full[block(k), block(j)] = full[block(j), block(k)].T
    for k, j in sorted(need_full):
        if abs(k - j) > width:
            full[block(k), block(j)] = jnp.zeros((size, size), BF16)
    for i, k in sorted(need_left):
        if abs(i - k) > width:
            piece = jnp.zeros((half, size), BF16)
        elif k >= i:
            piece = mine_ref[i, k - i]
        else:
            piece = full[pl.ds(i * size + mine, half), block(k)]
        left[pl.ds(i * half, half), block(k)] = piece

    sign = jnp.where(flag_ref[0] == 1, 1.0, -1.0)
    twice = jnp.where(flag_ref[0] == 1, 0.0, 2.0)
    copies = []
    for cols, i_lo, i_hi, k_lo, k_hi in jobs:
        depth = pl.ds(k_lo * size, (k_hi - k_lo + 1) * size)
        square = jnp.dot(
            left[pl.ds(i_lo * half, (i_hi - i_lo + 1) * half), depth],
            full[depth, pl.ds(cols[0] * size, len(cols) * size)],
            preferred_element_type=F32,
        )
        for i in range(i_lo, i_hi + 1):
            for d in [j - i for j in cols if 0 <= j - i <= width]:
                n = i + d - cols[0]
                kept = is_kept(reach_ref, i, d, first_row, total_rows)
                part = square[(i - i_lo) * half : (i - i_lo + 1) * half, n * size : (n + 1) * size]
                out_ref[i, d] = part * jnp.where(kept, sign, 0.0) + twice * mine_ref[i, d].astype(F32)
                if d == width:
                    copies.append(pltpu.make_async_copy(out_ref.at[i], out_hbm.at[i], sems.at[i]))
                    copies[-1].start()
    for copy in copies:
        copy.wait()


def fetch(base_ref, held, jobs, sems):
    copies = []
    for n, (row, d, count, at) in enumerate(jobs):
        copies.append(pltpu.make_async_copy(base_ref.at[row, pl.ds(d, count)], held.at[pl.ds(at, count)], sems.at[n]))
        copies[-1].start()
    return copies


def finish(dims, reach_ref, sign, square, from_row, from_col, copies, jobs, held, out_ref, sems):
    rows, width, half, size = dims
    first_row = lax.axis_index("row") * rows
    total_rows = lax.axis_size("row") * rows
    backs = []
    for n, (row, d, count, at) in enumerate(jobs):
        copies[n].wait()
        for e in range(count):
            i, j = row - from_row, row + d + e - from_col
            kept = is_kept(reach_ref, row, d + e, first_row, total_rows)
            part = square[i * half : (i + 1) * half, j * size : (j + 1) * size]
            held[at + e] = held[at + e] + part * jnp.where(kept, sign, 0.0)
        copy = pltpu.make_async_copy(held.at[pl.ds(at, count)], out_ref.at[row, pl.ds(d, count)], sems.at[n])
        copy.start()
        backs.append(copy)
    for copy in backs:
        copy.wait()


def halves(dims):
    half = dims[2]
    column = lax.axis_index("col")
    return pl.multiple_of(column * half, half), pl.multiple_of((1 - column) * half, half)


def add_above(dims, reach_ref, flag_ref, mine_ref, other_ref, base_ref, out_ref, whole, turned, left, held, in_sems, out_sems):
    rows, width, half, size = dims
    mine, other = halves(dims)
    jobs = runs(head_blocks(width))
    copies = fetch(base_ref, held, jobs, in_sems)

    def block(n):
        return pl.ds(n * size, size)

    have = set()
    for n, (row, d) in enumerate(tail_blocks(rows, width)):
        k, j = row - rows + width, row + d - rows
        whole[pl.ds(k * size + mine, half), block(j)] = mine_ref[n]
        whole[pl.ds(k * size + other, half), block(j)] = other_ref[n]
        have.add((k, j))
    for k in range(width):
        for j in range(width):
            if (k, j) in have:
                turned[block(j), block(k)] = whole[block(k), block(j)].T
                left[pl.ds(j * half, half), block(k)] = turned[pl.ds(j * size + mine, half), block(k)]
            else:
                whole[block(k), block(j)] = jnp.zeros((size, size), BF16)
                left[pl.ds(j * half, half), block(k)] = jnp.zeros((half, size), BF16)
    square = jnp.dot(left[...], whole[...], preferred_element_type=F32)
    sign = jnp.where(lax.axis_index("row") == 0, 0.0, jnp.where(flag_ref[0] == 1, 1.0, -1.0))
    finish(dims, reach_ref, sign, square, 0, 0, copies, jobs, held, out_ref, out_sems)


def add_below(dims, reach_ref, flag_ref, mine_ref, other_ref, sent_ref, base_ref, out_ref, whole, left, held, in_sems, out_sems):
    rows, width, half, size = dims
    mine, other = halves(dims)
    jobs = runs(tail_blocks(rows, width))
    copies = fetch(base_ref, held, jobs, in_sems)

    def block(n):
        return pl.ds(n * size, size)

    have = set()
    for n, (row, d) in enumerate(tail_blocks(rows, width)):
        i, k = row - rows + width, row + d - rows
        left[pl.ds(i * half, half), block(k)] = sent_ref[n]
        have.add((i, k))
    for i in range(width):
        for k in range(width):
            if (i, k) not in have:
                left[pl.ds(i * half, half), block(k)] = jnp.zeros((half, size), BF16)
    for n, (k, d) in enumerate(head_blocks(width)):
        whole[pl.ds(k * size + mine, half), block(k + d)] = mine_ref[n]
        whole[pl.ds(k * size + other, half), block(k + d)] = other_ref[n]
        if d:
            whole[block(k + d), block(k)] = whole[block(k), block(k + d)].T
    square = jnp.dot(left[...], whole[...], preferred_element_type=F32)
    sign = jnp.where(flag_ref[0] == 1, 1.0, -1.0)
    finish(dims, reach_ref, sign, square, rows - width, rows, copies, jobs, held, out_ref, out_sems)


def halo_kernel(
    dims, above_parity, reach_ref, flag_ref, mine_ref, other_ref, sent_ref, trace_ref, got_ref, base_ref, out_ref, sum_ref,
    whole, turned, left, held, sems,
):
    total = jnp.sum(trace_ref[...] + got_ref[...])
    if above_parity == 0:
        last = mine_ref.shape[0] - 1
        total = total + jnp.sum(mine_ref[last].astype(F32) + other_ref[last].astype(F32))
    sum_ref[0] = total / (lax.axis_size("row") * dims[0] * dims[3])
    parity = lax.axis_index("row") % 2

    @pl.when(parity == above_parity)
    def _():
        add_above(
            dims, reach_ref, flag_ref, mine_ref, other_ref, base_ref, out_ref, whole, turned, left, held, sems.at[0], sems.at[1]
        )

    @pl.when(parity != above_parity)
    def _():
        add_below(
            dims, reach_ref, flag_ref, mine_ref, other_ref, sent_ref, base_ref, out_ref, whole, left, held, sems.at[0], sems.at[1]
        )


def per_device(hamiltonian, bounds, block_reach, branch_flags):
    rows, offsets, half, size = hamiltonian.shape
    width = offsets - 1
    dims = (rows, width, half, size)
    halo = len(head_blocks(width))
    count = lax.axis_size("row")
    near_pairs = [(i, i ^ 1) for i in range(count)]
    far_pairs = [(i, j) for i in range(count) for j in [(((i + 1) ^ 1) - 1) % count]]
    swap = [(0, 1), (1, 0)]
    whole = jax.ShapeDtypeStruct(hamiltonian.shape, F32)
    packed = jax.ShapeDtypeStruct((halo, half, size), BF16)

    current, near, part = pl.pallas_call(
        functools.partial(start_kernel, dims),
        out_shape=(
            jax.ShapeDtypeStruct(hamiltonian.shape, BF16),
            packed,
            jax.ShapeDtypeStruct((LINES, size), F32),
        ),
        in_specs=[HBM, HBM, HBM, HBM],
        out_specs=(VMEM, VMEM, VMEM),
        scratch_shapes=[
            pltpu.VMEM(hamiltonian.shape, F32),
            pltpu.SMEM(block_reach.shape, jnp.int32),
            pltpu.SMEM(bounds.shape, F32),
            pltpu.SMEM(branch_flags.shape, jnp.int32),
            pltpu.SemaphoreType.DMA((rows,)),
            pltpu.SemaphoreType.DMA((3,)),
        ],
        compiler_params=pltpu.CompilerParams(vmem_limit_bytes=51 * MIB),
        cost_estimate=SMALL,
        name="start",
    )(block_reach, bounds, branch_flags, hamiltonian)
    swapped = lax.ppermute(current, "col", swap)
    near_mine = lax.ppermute(near, "row", near_pairs)
    steps = [1 << n for n in reversed(range(1, count.bit_length() - 1))]
    trace = part
    for step in steps:
        trace = trace + lax.ppermute(trace, "row", [(i, i ^ step) for i in range(count)])
    far = pl.pallas_call(
        functools.partial(pack_far_kernel, dims),
        out_shape=jax.ShapeDtypeStruct((halo + 1, half, size), BF16),
        in_specs=[VMEM, VMEM],
        out_specs=VMEM,
        compiler_params=pltpu.CompilerParams(vmem_limit_bytes=8 * MIB),
        cost_estimate=SMALL,
        name="pack_far",
    )(current, trace)
    got = lax.ppermute(trace, "col", swap)
    far_mine = lax.ppermute(far, "row", far_pairs)
    base = pl.pallas_call(
        functools.partial(inner_kernel, dims),
        out_shape=whole,
        in_specs=[SMEM, SMEM, VMEM, VMEM],
        out_specs=HBM,
        scratch_shapes=[
            pltpu.VMEM(hamiltonian.shape, F32),
            pltpu.VMEM(((rows + width) * size, (rows + width) * size), BF16),
            pltpu.VMEM((rows * half, (rows + width) * size), BF16),
            pltpu.SemaphoreType.DMA((rows,)),
        ],
        compiler_params=pltpu.CompilerParams(vmem_limit_bytes=24 * MIB),
        cost_estimate=SMALL,
        name="inner",
    )(block_reach, branch_flags, current, swapped)
    base, near_mine = lax.optimization_barrier((base, near_mine))
    near_other = lax.ppermute(near_mine, "col", swap)

    def add_halo(above_parity, mine, other, sent, trace, got, base):
        square = pltpu.VMEM((width * size, width * size), BF16)
        return pl.pallas_call(
            functools.partial(halo_kernel, dims, above_parity),
            out_shape=(whole, jax.ShapeDtypeStruct((1,), F32)),
            in_specs=[SMEM, SMEM, VMEM, VMEM, VMEM, VMEM, VMEM, ANY],
            out_specs=(ANY, SMEM),
            input_output_aliases={7: 0},
            scratch_shapes=[
                square, square, pltpu.VMEM((width * half, width * size), BF16), pltpu.VMEM((halo, half, size), F32),
                pltpu.SemaphoreType.DMA((2, width)),
            ],
            compiler_params=pltpu.CompilerParams(vmem_limit_bytes=16 * MIB),
            cost_estimate=SMALL,
            name="halo",
        )(block_reach, branch_flags, mine, other, sent, trace, got, base)

    base = add_halo(1, near_mine, near_other, near, trace, got, base)[0]
    base, far_mine = lax.optimization_barrier((base, far_mine))
    far_other = lax.ppermute(far_mine, "col", swap)
    return add_halo(0, far_mine, far_other, far, trace, got, base)


def solution(mesh):
    placed = (
        P(("groups", "row"), None, "col", None),
        P("groups"),
        P(("groups", "row")),
        P("groups"),
    )
    return jax.shard_map(
        per_device,
        mesh=mesh,
        in_specs=placed,
        out_specs=(P(("groups", "row"), None, "col", None), P("groups")),
        check_vma=False,
    )
```

```python
import functools

import jax
import jax.numpy as jnp
from jax import lax
from jax.experimental import pallas as pl
from jax.experimental.pallas import tpu as pltpu
from jax.sharding import PartitionSpec as P

SMEM = pl.BlockSpec(memory_space=pltpu.SMEM)
VMEM = pl.BlockSpec(memory_space=pltpu.VMEM)
ANY = pl.BlockSpec(memory_space=pl.ANY)
HBM = pl.BlockSpec(memory_space=pltpu.HBM)
F32 = jnp.float32
BF16 = jnp.bfloat16
MIB = 1 << 20
LINES = 16
SMALL = pl.CostEstimate(flops=1, bytes_accessed=1, transcendentals=0)


def tail_blocks(rows, width):
    return [(rows - m, d) for m in range(1, width + 1) for d in range(m, width + 1)]


def head_blocks(width):
    return [(m, d) for m in range(width) for d in range(width - m)]


def runs(blocks):
    out = []
    for place, (row, d) in enumerate(blocks):
        if out and out[-1][0] == row:
            out[-1][2] += 1
        else:
            out.append([row, d, 1, place])
    return out


def is_kept(reach_ref, row, d, first_row, total_rows):
    return (d <= reach_ref[row]) & (first_row + row + d < total_rows)


def start_block(h, d, kept, bounds_ref, on_diag):
    high = bounds_ref[1]
    scale = jnp.where(kept, 1.0, 0.0) / (high + bounds_ref[0])
    if d == 0:
        return ((jnp.where(on_diag, high, 0.0) - h) * scale).astype(BF16)
    return (h * -scale).astype(BF16)


def diag_mask(half, size):
    rows = lax.broadcasted_iota(jnp.int32, (half, size), 0) + lax.axis_index("col") * half
    return lax.broadcasted_iota(jnp.int32, (half, size), 1) == rows


def pack_halo(dims, tail_parity, x_ref, out_ref):
    rows, width = dims[:2]
    for parity in (0, 1):

        @pl.when(lax.axis_index("row") % 2 == parity)
        def _(parity=parity):
            blocks = tail_blocks(rows, width) if parity == tail_parity else head_blocks(width)
            for n, (row, d) in enumerate(blocks):
                out_ref[n] = x_ref[row, d]


def pack_far_kernel(dims, x_ref, sum_ref, out_ref):
    rows, width, half, size = dims
    pack_halo(dims, 1, x_ref, out_ref)
    rest = sum_ref[...]
    for n in range(half // LINES):
        term = rest.astype(BF16) if n < 3 else jnp.zeros((LINES, size), BF16)
        out_ref[out_ref.shape[0] - 1, pl.ds(n * LINES, LINES)] = term
        rest = rest - term.astype(F32)


def start_kernel(
    dims, reach_hbm, bounds_hbm, flag_hbm, h_hbm, x_ref, near_ref, part_ref, h_ref, reach_ref, bounds_ref,
    flag_ref, in_sems, small_sems,
):
    rows, width, half, size = dims
    first_row = lax.axis_index("row") * rows
    total_rows = lax.axis_size("row") * rows
    small = [
        pltpu.make_async_copy(src, dst, small_sems.at[n])
        for n, (src, dst) in enumerate(((reach_hbm, reach_ref), (bounds_hbm, bounds_ref), (flag_hbm, flag_ref)))
    ]
    large = [pltpu.make_async_copy(h_hbm.at[i], h_ref.at[i], in_sems.at[i]) for i in range(rows)]
    for copy in small + large:
        copy.start()
    on_diag = diag_mask(half, size)

    def fold(block):
        return jnp.sum(block.reshape(half // LINES, LINES, size), axis=0)

    for copy in small:
        copy.wait()
    diag = jnp.zeros((LINES, size), F32)
    once = jnp.zeros((LINES, size), F32)
    twice = jnp.zeros((LINES, size), F32)
    for row in range(rows):
        large[row].wait()
        for d in range(width + 1):
            kept = is_kept(reach_ref, row, d, first_row, total_rows)
            x = start_block(h_ref[row, d], d, kept, bounds_ref, on_diag)
            x_ref[row, d] = x
            wide = x.astype(F32)
            if d == 0:
                diag = diag + fold(jnp.where(on_diag, wide, 0.0))
                once = once + fold(wide * wide)
            else:
                twice = twice + fold(wide * wide)
    norm = once + 2.0 * twice
    part = jnp.where(flag_ref[0] == 1, norm, 2.0 * diag - norm)
    part_ref[...] = part

    pack_halo(dims, 0, x_ref, near_ref)

def strips(rows, width):
    out = []
    for j in range(0, rows + width, 2):
        cols = list(range(j, min(j + 2, rows + width)))
        i_lo, i_hi = max(0, j - width), min(rows - 1, cols[-1])
        k_lo = max(0, j - width)
        k_hi = min(rows + width - 1 if j < rows else rows - 1, cols[-1] + width, i_hi + width)
        out.append((cols, i_lo, i_hi, k_lo, k_hi))
    return out


def inner_kernel(dims, reach_ref, flag_ref, mine_ref, other_ref, out_hbm, out_ref, full, left, sems):
    rows, width, half, size = dims
    column = lax.axis_index("col")
    first_row = lax.axis_index("row") * rows
    total_rows = lax.axis_size("row") * rows
    mine = pl.multiple_of(column * half, half)
    other = pl.multiple_of((1 - column) * half, half)
    jobs = strips(rows, width)

    def block(n):
        return pl.ds(n * size, size)

    need_full, need_left = set(), set()
    for cols, i_lo, i_hi, k_lo, k_hi in jobs:
        need_full |= {(k, j) for k in range(k_lo, k_hi + 1) for j in cols}
        need_left |= {(i, k) for i in range(i_lo, i_hi + 1) for k in range(k_lo, k_hi + 1)}
    below = {(k, j) for k, j in need_full if j < k <= j + width}
    turned = below | {(i, k) for i, k in need_left if k < i <= k + width}
    for k, j in sorted({(k, j) for k, j in need_full if k <= j <= k + width} | {(j, k) for k, j in turned}):
        full[pl.ds(k * size + mine, half), block(j)] = mine_ref[k, j - k]
        full[pl.ds(k * size + other, half), block(j)] = other_ref[k, j - k]
    for k, j in sorted(turned):
        full[block(k), block(j)] = full[block(j), block(k)].T
    for k, j in sorted(need_full):
        if abs(k - j) > width:
            full[block(k), block(j)] = jnp.zeros((size, size), BF16)
    for i, k in sorted(need_left):
        if abs(i - k) > width:
            piece = jnp.zeros((half, size), BF16)
        elif k >= i:
            piece = mine_ref[i, k - i]
        else:
            piece = full[pl.ds(i * size + mine, half), block(k)]
        left[pl.ds(i * half, half), block(k)] = piece

    sign = jnp.where(flag_ref[0] == 1, 1.0, -1.0)
    twice = jnp.where(flag_ref[0] == 1, 0.0, 2.0)
    copies = []
    for cols, i_lo, i_hi, k_lo, k_hi in jobs:
        depth = pl.ds(k_lo * size, (k_hi - k_lo + 1) * size)
        square = jnp.dot(
            left[pl.ds(i_lo * half, (i_hi - i_lo + 1) * half), depth],
            full[depth, pl.ds(cols[0] * size, len(cols) * size)],
            preferred_element_type=F32,
        )
        for i in range(i_lo, i_hi + 1):
            for d in [j - i for j in cols if 0 <= j - i <= width]:
                n = i + d - cols[0]
                kept = is_kept(reach_ref, i, d, first_row, total_rows)
                part = square[(i - i_lo) * half : (i - i_lo + 1) * half, n * size : (n + 1) * size]
                out_ref[i, d] = part * jnp.where(kept, sign, 0.0) + twice * mine_ref[i, d].astype(F32)
                if d == width:
                    copies.append(pltpu.make_async_copy(out_ref.at[i], out_hbm.at[i], sems.at[i]))
                    copies[-1].start()
    for copy in copies:
        copy.wait()


def fetch(base_ref, held, jobs, sems):
    copies = []
    for n, (row, d, count, at) in enumerate(jobs):
        copies.append(pltpu.make_async_copy(base_ref.at[row, pl.ds(d, count)], held.at[pl.ds(at, count)], sems.at[n]))
        copies[-1].start()
    return copies


def finish(dims, reach_ref, sign, squares, from_row, from_col, from_pair, copies, jobs, held, out_ref, sems):
    rows, width, half, size = dims
    first_row = lax.axis_index("row") * rows
    total_rows = lax.axis_size("row") * rows
    backs = []
    for n, (row, d, count, at) in enumerate(jobs):
        copies[n].wait()
        for e in range(count):
            i, j = row - from_row, row + d + e - from_col
            kept = is_kept(reach_ref, row, d + e, first_row, total_rows)
            pair = j - j % 2
            i, j = i - pair * from_pair, j - pair
            part = squares[pair][i * half : (i + 1) * half, j * size : (j + 1) * size]
            held[at + e] = held[at + e] + part * jnp.where(kept, sign, 0.0)
        copy = pltpu.make_async_copy(held.at[pl.ds(at, count)], out_ref.at[row, pl.ds(d, count)], sems.at[n])
        copy.start()
        backs.append(copy)
    for copy in backs:
        copy.wait()


def halves(dims):
    half = dims[2]
    column = lax.axis_index("col")
    return pl.multiple_of(column * half, half), pl.multiple_of((1 - column) * half, half)


def add_above(dims, reach_ref, flag_ref, mine_ref, other_ref, base_ref, out_ref, whole, turned, left, held, in_sems, out_sems):
    rows, width, half, size = dims
    mine, other = halves(dims)
    jobs = runs(head_blocks(width))
    copies = fetch(base_ref, held, jobs, in_sems)

    def block(n):
        return pl.ds(n * size, size)

    have = set()
    for n, (row, d) in enumerate(tail_blocks(rows, width)):
        k, j = row - rows + width, row + d - rows
        whole[pl.ds(k * size + mine, half), block(j)] = mine_ref[n]
        whole[pl.ds(k * size + other, half), block(j)] = other_ref[n]
        have.add((k, j))
    for k in range(width):
        for j in range(width):
            if (k, j) in have:
                turned[block(j), block(k)] = whole[block(k), block(j)].T
                left[pl.ds(j * half, half), block(k)] = turned[pl.ds(j * size + mine, half), block(k)]
            elif k >= j - j % 2:
                whole[block(k), block(j)] = jnp.zeros((size, size), BF16)
                left[pl.ds(j * half, half), block(k)] = jnp.zeros((half, size), BF16)
    squares = {}
    for j in range(0, width, 2):
        depth, cols = pl.ds(j * size, (width - j) * size), min(2, width - j)
        squares[j] = jnp.dot(
            left[pl.ds(0, (j + cols) * half), depth],
            whole[depth, pl.ds(j * size, cols * size)],
            preferred_element_type=F32,
        )
    sign = jnp.where(lax.axis_index("row") == 0, 0.0, jnp.where(flag_ref[0] == 1, 1.0, -1.0))
    finish(dims, reach_ref, sign, squares, 0, 0, False, copies, jobs, held, out_ref, out_sems)


def add_below(dims, reach_ref, flag_ref, mine_ref, other_ref, sent_ref, base_ref, out_ref, whole, left, held, in_sems, out_sems):
    rows, width, half, size = dims
    mine, other = halves(dims)
    jobs = runs(tail_blocks(rows, width))
    copies = fetch(base_ref, held, jobs, in_sems)

    def block(n):
        return pl.ds(n * size, size)

    have = set()
    for n, (row, d) in enumerate(tail_blocks(rows, width)):
        i, k = row - rows + width, row + d - rows
        left[pl.ds(i * half, half), block(k)] = sent_ref[n]
        have.add((i, k))
    for i in range(width):
        for k in range(width):
            if (i, k) not in have:
                left[pl.ds(i * half, half), block(k)] = jnp.zeros((half, size), BF16)
    for n, (k, d) in enumerate(head_blocks(width)):
        whole[pl.ds(k * size + mine, half), block(k + d)] = mine_ref[n]
        whole[pl.ds(k * size + other, half), block(k + d)] = other_ref[n]
        if d:
            whole[block(k + d), block(k)] = whole[block(k), block(k + d)].T
    squares = {}
    for j in range(0, width, 2):
        cols = min(2, width - j)
        squares[j] = jnp.dot(
            left[pl.ds(j * half, (width - j) * half), :],
            whole[:, pl.ds(j * size, cols * size)],
            preferred_element_type=F32,
        )
    sign = jnp.where(flag_ref[0] == 1, 1.0, -1.0)
    finish(dims, reach_ref, sign, squares, rows - width, rows, True, copies, jobs, held, out_ref, out_sems)


def halo_kernel(
    dims, above_parity, reach_ref, flag_ref, mine_ref, other_ref, sent_ref, trace_ref, got_ref, base_ref, out_ref, sum_ref,
    whole, turned, left, held, sems,
):
    total = jnp.sum(trace_ref[...] + got_ref[...])
    if above_parity == 0:
        last = mine_ref.shape[0] - 1
        total = total + jnp.sum(mine_ref[last].astype(F32) + other_ref[last].astype(F32))
    sum_ref[0] = total / (lax.axis_size("row") * dims[0] * dims[3])
    parity = lax.axis_index("row") % 2

    @pl.when(parity == above_parity)
    def _():
        add_above(
            dims, reach_ref, flag_ref, mine_ref, other_ref, base_ref, out_ref, whole, turned, left, held, sems.at[0], sems.at[1]
        )

    @pl.when(parity != above_parity)
    def _():
        add_below(
            dims, reach_ref, flag_ref, mine_ref, other_ref, sent_ref, base_ref, out_ref, whole, left, held, sems.at[0], sems.at[1]
        )


def per_device(hamiltonian, bounds, block_reach, branch_flags):
    rows, offsets, half, size = hamiltonian.shape
    width = offsets - 1
    dims = (rows, width, half, size)
    halo = len(head_blocks(width))
    count = lax.axis_size("row")
    near_pairs = [(i, i ^ 1) for i in range(count)]
    far_pairs = [(i, j) for i in range(count) for j in [(((i + 1) ^ 1) - 1) % count]]
    swap = [(0, 1), (1, 0)]
    whole = jax.ShapeDtypeStruct(hamiltonian.shape, F32)
    packed = jax.ShapeDtypeStruct((halo, half, size), BF16)

    current, near, part = pl.pallas_call(
        functools.partial(start_kernel, dims),
        out_shape=(
            jax.ShapeDtypeStruct(hamiltonian.shape, BF16),
            packed,
            jax.ShapeDtypeStruct((LINES, size), F32),
        ),
        in_specs=[HBM, HBM, HBM, HBM],
        out_specs=(VMEM, VMEM, VMEM),
        scratch_shapes=[
            pltpu.VMEM(hamiltonian.shape, F32),
            pltpu.SMEM(block_reach.shape, jnp.int32),
            pltpu.SMEM(bounds.shape, F32),
            pltpu.SMEM(branch_flags.shape, jnp.int32),
            pltpu.SemaphoreType.DMA((rows,)),
            pltpu.SemaphoreType.DMA((3,)),
        ],
        compiler_params=pltpu.CompilerParams(vmem_limit_bytes=51 * MIB),
        cost_estimate=SMALL,
        name="start",
    )(block_reach, bounds, branch_flags, hamiltonian)
    swapped = lax.ppermute(current, "col", swap)
    near_mine = lax.ppermute(near, "row", near_pairs)
    steps = [1 << n for n in reversed(range(1, count.bit_length() - 1))]
    trace = part
    for step in steps:
        trace = trace + lax.ppermute(trace, "row", [(i, i ^ step) for i in range(count)])
    far = pl.pallas_call(
        functools.partial(pack_far_kernel, dims),
        out_shape=jax.ShapeDtypeStruct((halo + 1, half, size), BF16),
        in_specs=[VMEM, VMEM],
        out_specs=VMEM,
        compiler_params=pltpu.CompilerParams(vmem_limit_bytes=8 * MIB),
        cost_estimate=SMALL,
        name="pack_far",
    )(current, trace)
    got = lax.ppermute(trace, "col", swap)
    far_mine = lax.ppermute(far, "row", far_pairs)
    swapped, near_mine = lax.optimization_barrier((swapped, near_mine))
    base = pl.pallas_call(
        functools.partial(inner_kernel, dims),
        out_shape=whole,
        in_specs=[SMEM, SMEM, VMEM, VMEM],
        out_specs=HBM,
        scratch_shapes=[
            pltpu.VMEM(hamiltonian.shape, F32),
            pltpu.VMEM(((rows + width) * size, (rows + width) * size), BF16),
            pltpu.VMEM((rows * half, (rows + width) * size), BF16),
            pltpu.SemaphoreType.DMA((rows,)),
        ],
        compiler_params=pltpu.CompilerParams(vmem_limit_bytes=24 * MIB),
        cost_estimate=SMALL,
        name="inner",
    )(block_reach, branch_flags, current, swapped)
    near_other = lax.ppermute(near_mine, "col", swap)

    def add_halo(above_parity, mine, other, sent, trace, got, base):
        square = pltpu.VMEM((width * size, width * size), BF16)
        return pl.pallas_call(
            functools.partial(halo_kernel, dims, above_parity),
            out_shape=(whole, jax.ShapeDtypeStruct((1,), F32)),
            in_specs=[SMEM, SMEM, VMEM, VMEM, VMEM, VMEM, VMEM, ANY],
            out_specs=(ANY, SMEM),
            input_output_aliases={7: 0},
            scratch_shapes=[
                square, square, pltpu.VMEM((width * half, width * size), BF16), pltpu.VMEM((halo, half, size), F32),
                pltpu.SemaphoreType.DMA((2, width)),
            ],
            compiler_params=pltpu.CompilerParams(vmem_limit_bytes=16 * MIB),
            cost_estimate=SMALL,
            name="halo",
        )(block_reach, branch_flags, mine, other, sent, trace, got, base)

    base = add_halo(1, near_mine, near_other, near, trace, got, base)[0]
    base, far_mine = lax.optimization_barrier((base, far_mine))
    far_other = lax.ppermute(far_mine, "col", swap)
    return add_halo(0, far_mine, far_other, far, trace, got, base)


def solution(mesh):
    placed = (
        P(("groups", "row"), None, "col", None),
        P("groups"),
        P(("groups", "row")),
        P("groups"),
    )
    return jax.shard_map(
        per_device,
        mesh=mesh,
        in_specs=placed,
        out_specs=(P(("groups", "row"), None, "col", None), P("groups")),
        check_vma=False,
    )
```
